512 devices in a mesh: section: 8 (over z_lo, core), seq: 64 (over y, z_hi, x).
Axes of the slice: x: 4, y: 4, z: 16 (z_hi: 4, z_lo: 4; z = z_hi * 4 + z_lo), core: 2. Of those that a mesh axis runs over, the one named last changes fastest.
Arguments:
- x_saved: bfloat16 [8, 2, 8192, 1024], P('section', None, 'seq'), may hold values from -6 to 6
- queries: bfloat16 [8, 2, 8192, 1024], P('section', None, 'seq'), may hold values from -30 to 30
- keys: bfloat16 [8, 2, 8192, 1024], P('section', None, 'seq'), may hold values from -30 to 30
- value_weight: bfloat16 [8, 1024, 1024], P('section', 'seq'), may hold values from -0.1875 to 0.1875
- out_weight: bfloat16 [8, 1024, 1024], P('section', 'seq'), may hold values from -0.1875 to 0.1875
- out_grad: bfloat16 [2, 8192, 1024], P(None, 'seq'), may hold values from -6 to 6
Outputs:
- section_grads: bfloat16 [8, 2, 8192, 1024], P('section', None, 'seq')
- query_grads: bfloat16 [8, 2, 8192, 1024], P('section', None, 'seq')
- key_grads: bfloat16 [8, 2, 8192, 1024], P('section', None, 'seq')
The draws below stay inside these ranges and needn't reach their ends.
All inputs are finite; a program needn't handle non-finite values.
Results may differ from the reference program's by a relative error of at most 0.025.
Values may be sent and summed in bfloat16 or wider, within the bound.
A program may use at most 128 MiB of HBM per device.

```python
import math
import jax
import jax.numpy as jnp
from jax import lax

D = 1024
HEADS = 8
HEAD = 128
MICRO = 2
ROWS = 128
INNER = 1024
SECTIONS = 8
SEQ_LEN = 8192


def draw_queries(key, part):
    key = jax.random.fold_in(key, 1)
    shape = (SECTIONS, MICRO, SEQ_LEN, INNER)
    own = jax.random.normal(key, shape, jnp.float32)
    return own.astype(jnp.bfloat16)


def draw_keys(key, part):
    key = jax.random.fold_in(key, 2)
    shape = (SECTIONS, MICRO, SEQ_LEN, INNER)
    own = jax.random.normal(key, shape, jnp.float32)
    return own.astype(jnp.bfloat16)


def levels(key, shape, split, least, high):
    level = 1.0
    for dim, shards_of in split:
        draws = jax.random.uniform(jax.random.fold_in(jax.random.fold_in(key, 6), dim), (shards_of,), jnp.float32, least / len(split), high / len(split))
        level = level * jnp.repeat(jnp.exp(draws), shape[dim] // shards_of).reshape((-1,) + (1,) * (len(shape) - 1 - dim))
    return level


def noise(stream_key, extent, spread, limit, pieces=(), kind=jnp.bfloat16):
    gain = levels(stream_key, extent, pieces, -0.22, 0.18) if pieces else 1.0
    result = jax.random.normal(stream_key, extent, jnp.float32) * spread * gain
    return jnp.minimum(jnp.maximum(result, -limit), limit).astype(kind)


def setup_inputs(seed: int = 0) -> dict:
    streams_of = jax.random.split(jax.random.key(seed), 7)
    x_saved = noise(streams_of[0], (SECTIONS, MICRO, SEQ_LEN, D), 1.0, 6.0, ((0, 8), (2, 64)))
    queries = draw_queries(jax.random.fold_in(streams_of[6], 71), 0)
    keys = draw_keys(jax.random.fold_in(streams_of[6], 71), 0)
    value_weight = noise(streams_of[3], (SECTIONS, D, INNER), D ** -0.5, 0.1875, ((0, 8), (1, 64)))
    out_weight = noise(streams_of[4], (SECTIONS, INNER, D), INNER ** -0.5, 0.1875, ((0, 8), (1, 64)))
    out_grad = noise(streams_of[5], (MICRO, SEQ_LEN, D), 1.0, 6.0, ((1, 64),))
    return {"x_saved": x_saved, "queries": queries, "keys": keys, "value_weight": value_weight, "out_weight": out_weight, "out_grad": out_grad}


def split_heads(array, block_count):
    return array.reshape(block_count, ROWS, HEADS, HEAD).astype(jnp.float32)

def with_previous(array, block_count):
    earlier = jnp.concatenate([jnp.zeros((ROWS, array.shape[1]), array.dtype), array[:-ROWS]], 0)
    return jnp.concatenate([split_heads(earlier, block_count), split_heads(array, block_count)], 1)

def fold_back(pairs, block_count):
    following = jnp.concatenate([pairs[1:, :ROWS], jnp.zeros((1, ROWS, HEADS, HEAD), jnp.float32)], 0)
    following = lax.optimization_barrier(following.astype(jnp.bfloat16)).astype(jnp.float32)
    return (pairs[:, ROWS:] + following).reshape(block_count * ROWS, HEADS * HEAD)

def backward_layer(x_rows, query_rows, key_rows, value_weight, out_weight, incoming):
    block_count = x_rows.shape[0] // ROWS
    score_scale = 1.0 / math.sqrt(HEAD)
    values = jnp.dot(x_rows, value_weight, preferred_element_type=jnp.float32).astype(jnp.bfloat16)
    value_grad_in = jnp.dot(incoming, out_weight.T, preferred_element_type=jnp.float32).astype(jnp.bfloat16)
    query_blocks = split_heads(query_rows, block_count)
    key_pairs = with_previous(key_rows, block_count)
    value_pairs = with_previous(values, block_count)
    grad_blocks = split_heads(value_grad_in, block_count)
    row_index = jnp.arange(ROWS)[:, None]
    col_index = jnp.arange(2 * ROWS)[None, :]
    own_mask = (col_index >= ROWS) & (col_index - ROWS <= row_index)
    prior_mask = (col_index < ROWS) & (col_index > row_index)
    block_index = jnp.arange(block_count)[:, None, None]
    allowed = (own_mask[None] | prior_mask[None] & (block_index > 0))[:, None]
    scores = jnp.einsum('brhd,bchd->bhrc', query_blocks, key_pairs) * score_scale
    scores = jnp.where(allowed, scores, -1e+30)
    row_max = lax.optimization_barrier(jnp.max(scores, axis=-1, keepdims=True))
    exponent = jnp.where(allowed, jnp.exp(scores - row_max), 0.0)
    probabilities = exponent / lax.optimization_barrier(jnp.sum(exponent, axis=-1, keepdims=True))
    prob_rounded = probabilities.astype(jnp.bfloat16).astype(jnp.float32)
    attended = jnp.einsum('bhrc,bchd->brhd', prob_rounded, value_pairs)
    row_delta = lax.optimization_barrier(jnp.sum(grad_blocks * attended, axis=-1))
    dprob = jnp.einsum('brhd,bchd->bhrc', grad_blocks, value_pairs)
    score_grad = probabilities * (dprob - jnp.transpose(row_delta, (0, 2, 1))[..., None]) * score_scale
    score_rounded = score_grad.astype(jnp.bfloat16).astype(jnp.float32)
    query_grad = jnp.einsum('bhrc,bchd->brhd', score_rounded, key_pairs).reshape(block_count * ROWS, HEADS * HEAD)
    key_grad = fold_back(jnp.einsum('bhrc,brhd->bchd', score_rounded, query_blocks), block_count)
    value_grad = fold_back(jnp.einsum('bhrc,brhd->bchd', prob_rounded, grad_blocks), block_count)
    input_part = jnp.dot(value_grad.astype(jnp.bfloat16), value_weight.T, preferred_element_type=jnp.float32)
    return (query_grad.astype(jnp.bfloat16), key_grad.astype(jnp.bfloat16), input_part)

def reference(x_saved, queries, keys, value_weight, out_weight, out_grad):
    section_count = queries.shape[0]
    grads_list = [None] * section_count
    query_list = [None] * section_count
    key_list = [None] * section_count
    current = out_grad
    for section_index in reversed(range(section_count)):
        results = []
        query_parts = []
        key_parts = []
        for micro_index in range(MICRO):
            x_rows = x_saved[section_index, micro_index]
            if section_index >= section_count // 2:
                x_rows = (x_rows.astype(jnp.float32) + x_saved[section_count - 1 - section_index, micro_index].astype(jnp.float32)).astype(jnp.bfloat16)
            query_part, key_part, input_part = backward_layer(x_rows, queries[section_index, micro_index], keys[section_index, micro_index], value_weight[section_index], out_weight[section_index], current[micro_index])
            summed = current[micro_index].astype(jnp.float32) + input_part
            if section_index < section_count // 2:
                summed = summed + grads_list[section_count - 1 - section_index][micro_index].astype(jnp.float32)
            results.append(summed.astype(jnp.bfloat16))
            query_parts.append(query_part)
            key_parts.append(key_part)
        current = jnp.stack(results)
        grads_list[section_index] = current
        query_list[section_index] = jnp.stack(query_parts)
        key_list[section_index] = jnp.stack(key_parts)
    return (jnp.stack(grads_list), jnp.stack(query_list), jnp.stack(key_list))
```

```python
import functools
import math

import jax
import jax.numpy as jnp
from jax import lax
from jax.experimental import pallas as pl
from jax.experimental.pallas import tpu as pltpu
from jax.sharding import PartitionSpec as P

MESH = pl.DeviceIdType.MESH
HEADS = 8
HEAD = 128
ROWS = 128
SIDE = 4
CHUNKS = 4
BF16 = jnp.bfloat16
F32 = jnp.float32
NN = (((1,), (0,)), ((), ()))
NT = (((1,), (1,)), ((), ()))


def dot(left, right, dims=NN):
    return lax.dot_general(left, right, dims, preferred_element_type=F32)


def kernel(
    sections, blocks, width,
    x, q, k, wv, wo, og,
    sg, dq, dk,
    w, qv, kv, xv, ogv, qnext, kt, vals, xh, xmirror, weight, prob, grx, out, skip, acc, vgi, vg,
    stat, statrx, factor, bias, dprob, delta, deltarx, dqown, dqnext, dqrx, pass1, pass2,
    lsem, qsend, qrecv, e1send, e1recv, e2send, e2recv, e3send, e3recv, tsend, trecv, msend, mrecv, zsend, zrecv, rsend, rrecv, isend,
    gsend, grecv, ssend, srecv, esend, erecv, dsend, drecv, go_z, go_r,
):
    s = lax.axis_index("section")
    i = lax.axis_index("seq")
    cy = lax.div(i, SIDE * SIDE)
    cz = lax.rem(lax.div(i, SIDE), SIDE)
    cx = lax.rem(i, SIDE)
    after = lax.rem(i + 1, blocks)
    before = lax.rem(i + blocks - 1, blocks)
    top = sections - 1
    half = sections // 2
    mirror_s = top - s
    step = width // CHUNKS
    scale = 1.0 / math.sqrt(HEAD)

    def at(y, z, x_):
        return y * (SIDE * SIDE) + z * SIDE + x_

    def copy(src, dst, send, recv, device):
        return pltpu.make_async_remote_copy(
            src_ref=src, dst_ref=dst, send_sem=send, recv_sem=recv,
            device_id=device, device_id_type=MESH,
        )


    def local_copy(n):
        src, dst = (
            (q.at[0], qv), (k.at[0], kv), (wo.at[0], w.at[0, cy, cz, cx]),
            (wv.at[0], w.at[1, cy, cz, cx]), (x.at[0], xv), (og, ogv),
        )[n]
        return pltpu.make_async_copy(src, dst, lsem.at[n])

    def query_copy(m):
        return copy(q.at[0, m], qnext.at[m], qsend.at[m], qrecv.at[m], (s, before))


    quarter = ROWS // SIDE
    back = lax.rem(i + blocks - SIDE, blocks)

    def edge_out(j):
        src = q.at[0, :, pl.ds(j * quarter, quarter)]
        return copy(src, pass1, e1send.at[j], e1recv.at[0], (s, i + j))

    def edge_over(first, last):
        src = q.at[0, :, pl.ds(0, quarter)] if first else pass1
        if last:
            dst, sem = qnext.at[:, pl.ds((SIDE - 1) * quarter, quarter)], e3recv.at[SIDE - 1]
        else:
            dst, sem = pass2, e2recv.at[0]
        return copy(src, dst, e2send.at[0], sem, (s, back))

    def edge_in():
        rows = pl.ds(pl.multiple_of(cx * quarter, quarter), quarter)
        to = i - cx + SIDE - 1
        return copy(pass2, qnext.at[:, rows], e3send.at[0], e3recv.at[cx], (s, to))

    def edge_arrival(j):
        part = qnext.at[:, pl.ds(j * quarter, quarter)]
        return copy(part, part, e3send.at[0], e3recv.at[j], (s, i))

    def stat_copy(m, side):
        to = before if side == 0 else after
        return copy(
            stat.at[m, side], statrx.at[m, 1 - side], tsend.at[m, side], trecv.at[m, 1 - side], (s, to)
        )

    def delta_copy(m, side):
        to = before if side == 0 else after
        return copy(
            delta.at[m, side], deltarx.at[m, 1 - side], esend.at[m, side], erecv.at[m, 1 - side], (s, to)
        )

    def mirror_copy():
        return copy(x.at[0], xmirror, msend.at[0], mrecv.at[0], (mirror_s, i))

    def z_copy(a, d):
        to = at(cy, lax.rem(cz + d, SIDE), cx)
        src = (wo if a == 0 else wv).at[0]
        return copy(src, w.at[a, cy, cz, cx], zsend.at[a, d - 1], zrecv.at[a, d - 1], (s, to))

    def z_arrival(a, d):
        piece = w.at[a, cy, lax.rem(cz + SIDE - d, SIDE), cx]
        return copy(piece, piece, zsend.at[a, d - 1], zrecv.at[a, d - 1], (s, i))

    def slab(a, h, phase, c, part):
        zs = pl.ds(2 * h, 2) if part is None else 2 * h + part
        if phase == 0:
            return w.at[a, cy, zs, c] if h == 0 else w.at[a, c, zs, cx]
        return w.at[a, c, zs] if h == 0 else w.at[a, :, zs, c]

    def ring(a, h, phase, kind, arrival=False):
        along_x = phase == h
        me = cx if along_x else cy
        plus, minus = lax.rem(me + 1, SIDE), lax.rem(me + SIDE - 1, SIDE)
        across = lax.rem(me + 2, SIDE)
        part = None if kind < 2 else kind - 2
        if arrival:
            held = (minus, plus, across, across)[kind]
        else:
            held = (me, me, minus, plus)[kind]
        goes = plus if kind % 2 == 0 else minus
        to = at(cy, cz, goes) if along_x else at(goes, cz, cx)
        piece = slab(a, h, phase, held, part)
        sems = (a, h, phase, kind)
        return copy(piece, piece, rsend.at[sems], rrecv.at[sems], (s, to))

    def init_copy(m, c):
        return copy(
            grx.at[m, 0, c], grx.at[m, 1, c], isend.at[m, c], grecv.at[m, 1, c], (s, before)
        )

    def grad_copy(m, c, j):
        to = (s - 1, i) if j == 0 else (s - 1, before)
        return copy(out.at[m, c], grx.at[m, j, c], gsend.at[m, j, c], grecv.at[m, j, c], to)

    def skip_copy(m):
        return copy(out.at[m], skip.at[m], ssend.at[m], srecv.at[m], (mirror_s, i))

    def dq_copy(m):
        return copy(dqnext.at[m], dqrx.at[m], dsend.at[m], drecv.at[m], (s, after))

    for n in range(5):
        local_copy(n).start()

    @pl.when(s == top)
    def _():
        local_copy(5).start()


    barrier = pltpu.get_barrier_semaphore()

    def greet(section, seq):
        pl.semaphore_signal(barrier, inc=1, device_id=(section, seq), device_id_type=MESH)

    greet(s, after)
    greet(s, before)
    greet(mirror_s, i)
    for d in range(1, SIDE):
        greet(s, at(cy, lax.rem(cz + d, SIDE), cx))
        greet(s, at(cy, cz, lax.rem(cx + d, SIDE)))
    for d in (1, SIDE - 1):
        greet(s, at(lax.rem(cy + d, SIDE), cz, cx))
        greet(s, lax.rem(i + d * SIDE + (blocks - SIDE * SIDE if d > 1 else 0), blocks))

    @pl.when(s > 0)
    def _():
        greet(s - 1, i)
        greet(s - 1, before)

    @pl.when(s < top)
    def _():
        greet(s + 1, i)
        greet(s + 1, after)

    @pl.when(s > 1)
    def _():
        greet(s - 2, i)

    @pl.when(s < top - 1)
    def _():
        greet(s + 2, i)

    @pl.when((s == 0) | (s == top))
    def _():
        pl.semaphore_wait(barrier, 16)

    @pl.when((s == 1) | (s == top - 1))
    def _():
        pl.semaphore_wait(barrier, 18)

    @pl.when((s > 1) & (s < top - 1))
    def _():
        pl.semaphore_wait(barrier, 19)


    row = lax.broadcasted_iota(jnp.int32, (ROWS, 2 * ROWS), 0)
    col = lax.broadcasted_iota(jnp.int32, (ROWS, 2 * ROWS), 1)
    no_next = jnp.where(i == blocks - 1, 2 * ROWS, 0)
    allowed = ((col < ROWS) & (row <= col)) | ((col >= ROWS) & (row > col - ROWS + no_next))
    bias[...] = jnp.where(allowed, 0.0, -1e30)

    def each_head(body):
        for h in range(HEADS):
            body(h, slice(h * HEAD, (h + 1) * HEAD))

    def soft_in(m):
        @pl.when(cx < SIDE - 1)
        def _():
            query_copy(m).wait_recv()

        def head(h, cols):
            keys = kv[m, :, cols]
            queries = jnp.concatenate([qv[m, :, cols], qnext[m, :, cols]], 0)
            score = dot(keys, queries, NT) * scale + bias[...]
            high = jnp.maximum(jnp.max(score, axis=0, keepdims=True), -1e29)
            e = jnp.exp(score - high)
            total = jnp.sum(e, axis=0, keepdims=True)
            weight[m, h] = e
            one = slice(h, h + 1)
            stat[m, 0, 0, one] = high[:, :ROWS]
            stat[m, 1, 0, one] = high[:, ROWS:]
            stat[m, 0, 1, one] = total[:, :ROWS]
            stat[m, 1, 1, one] = total[:, ROWS:]
            kt[m, cols] = keys.T

        each_head(head)
        for side in range(2):
            stat_copy(m, side).start()

    def soft_out(m):
        for side in range(2):
            stat_copy(m, 1 - side).wait_recv()
            here, there = stat[m, side, 0], statrx[m, side, 0]
            high = jnp.maximum(here, there)
            mine = jnp.exp(here - high)
            total = stat[m, side, 1] * mine + statrx[m, side, 1] * jnp.exp(there - high)
            factor[side] = mine / total

        def head(h, cols):
            one = slice(h, h + 1)
            part = jnp.concatenate([factor[0, one], factor[1, one]], 1)
            prob[m, h] = (weight[m, h] * part).astype(BF16)

        each_head(head)

    def values():
        @pl.when(s >= half)
        def _():
            mirror_copy().wait_recv()
            xh[...] = (xv[...].astype(F32) + xmirror[...].astype(F32)).astype(BF16)

        @pl.when(s < half)
        def _():
            xh[...] = xv[...]

        def columns(c, carry):
            cols = pl.ds(pl.multiple_of(c * step, step), step)
            part = w[1, :, :, :, :, cols].reshape(width, step)
            result = dot(xh[...].reshape(2 * ROWS, width), part).astype(BF16)
            vals[:, :, cols] = result.reshape(2, ROWS, step)
            return carry

        lax.fori_loop(0, CHUNKS, columns, 0)

    def chain_in(m):
        acc[...] = jnp.zeros_like(acc)

        @pl.when((s < top) & (lax.rem(s, 2) == 0))
        def _():
            for c in range(CHUNKS):
                grad_copy(m, c, 0).wait_recv()

        @pl.when((s < top) & (lax.rem(s, 2) == 1))
        def _():
            for c in range(CHUNKS):
                grad_copy(m, c, 0).wait_recv()
                init_copy(m, c).start()

        def chunk(c, carry):
            grad_copy(m, c, 1).wait_recv()
            cols = pl.ds(pl.multiple_of(c * step, step), step)
            both = jnp.concatenate([grx[m, 0, c], grx[m, 1, c]], 1)
            part = w[0, :, :, :, :, cols].reshape(width, step)
            acc[...] += dot(part, both)
            return carry

        lax.fori_loop(0, CHUNKS, chunk, 0)
        vgi[m] = acc[...].astype(BF16)

    def chain_out(m):
        for h in range(HEADS):
            rows = slice(h * HEAD, (h + 1) * HEAD)
            vg[rows] = dot(vgi[m, rows], prob[m, h], NT).astype(BF16)

        @pl.when(s < half - 1)
        def _():
            skip_copy(m).wait_recv()

        @pl.when(s == half - 1)
        def _():
            skip[m] = grx[m, 0]

        def chunk(c, carry):
            part = w[1, c].reshape(step, width)
            total = dot(part, vg[...]) + grx[m, 0, c].astype(F32) + skip[m, c].astype(F32)
            out[m, c] = total.astype(BF16)

            @pl.when(lax.rem(s, 2) == 1)
            def _():
                grad_copy(m, c, 1).start()

            @pl.when(s > 0)
            def _():
                grad_copy(m, c, 0).start()

            return carry

        lax.fori_loop(0, CHUNKS, chunk, 0)

        @pl.when(s > half)
        def _():
            skip_copy(m).start()

    def post_in(m):
        def head(h, cols):
            grad = dot(vals[m, :, cols], vgi[m, cols])
            dprob[h] = grad
            total = jnp.sum(prob[m, h].astype(F32) * grad, axis=0, keepdims=True)
            one = slice(h, h + 1)
            delta[m, 0, one] = total[:, :ROWS]
            delta[m, 1, one] = total[:, ROWS:]

        each_head(head)
        for side in range(2):
            delta_copy(m, side).start()

    def post_out(m):
        for side in range(2):
            delta_copy(m, 1 - side).wait_recv()
            factor[side] = delta[m, side] + deltarx[m, side]

        def head(h, cols):
            one = slice(h, h + 1)
            whole = jnp.concatenate([factor[0, one], factor[1, one]], 1)
            ds = (prob[m, h].astype(F32) * (dprob[h] - whole) * scale).astype(BF16)
            queries = jnp.concatenate([qv[m, :, cols], qnext[m, :, cols]], 0)
            dk[0, m, :, cols] = dot(ds, queries).astype(BF16)
            both = dot(kt[m, cols], ds)
            dqown[m, cols] = both[:, :ROWS]
            dqnext[m, cols] = both[:, ROWS:].astype(BF16)

        each_head(head)
        dq_copy(m).start()


    @pl.when(s < top - 1)
    def _():
        pl.semaphore_wait(go_z, 1)

    @pl.when(cx == 0)
    def _():
        for j in range(1, SIDE):
            edge_out(j).start()
        edge_over(True, False).start()

    @pl.when(cx > 0)
    def _():
        for m in range(2):
            query_copy(m).start()

    for a in range(2):
        for d in range(1, SIDE):
            z_copy(a, d).start()

    for n in range(5):
        local_copy(n).wait()

    @pl.when(cx > 0)
    def _():
        edge_out(0).wait_recv()

    @pl.when((cx > 0) & (cx < SIDE - 1))
    def _():
        edge_over(False, False).start()

    @pl.when(cx == SIDE - 1)
    def _():
        edge_over(False, True).start()

    @pl.when(s == top)
    def _():
        local_copy(5).wait()
        for m in range(2):
            for c in range(CHUNKS):
                grx[m, 0, c] = ogv[m, :, c * step:(c + 1) * step].T
                init_copy(m, c).start()

    @pl.when(s >= half)
    def _():
        skip[...] = jnp.zeros_like(skip)

    for a in range(2):
        for d in range(1, SIDE):
            z_arrival(a, d).wait_recv()
        for h in range(2):
            for kind in range(2):
                ring(a, h, 0, kind).start()

    @pl.when(s > 1)
    def _():
        pl.semaphore_signal(go_z, inc=1, device_id=(s - 2, i), device_id_type=MESH)

    @pl.when(s < half)
    def _():
        mirror_copy().start()

    @pl.when(cx < SIDE - 1)
    def _():
        edge_over(False, False).wait_recv()
        edge_in().start()

    def relay(a, phase):
        for h in range(2):
            for kind in range(2):
                ring(a, h, phase, kind, True).wait_recv()
                ring(a, h, phase, kind + 2).start()

    def settle(a, phase):
        for h in range(2):
            for kind in range(2, 4):
                ring(a, h, phase, kind, True).wait_recv()

    def second():
        for a in range(2):
            settle(a, 0)
            for h in range(2):
                for kind in range(2):
                    ring(a, h, 1, kind).start()

    def each_micro(body):
        def turn(m, carry):
            body(m)
            return carry

        lax.fori_loop(0, 2, turn, 0)

    odd = lax.rem(s, 2) == 1
    for a in range(2):
        relay(a, 0)

    @pl.when(odd)
    def _():
        second()

    @pl.when(cx == SIDE - 1)
    def _():
        for j in range(SIDE):
            edge_arrival(j).wait_recv()

    each_micro(soft_in)

    @pl.when(odd)
    def _():
        for a in range(2):
            relay(a, 1)
        pl.semaphore_signal(go_r, inc=1, device_id=(s - 1, i), device_id_type=MESH)

    each_micro(soft_out)

    @pl.when(jnp.logical_not(odd))
    def _():
        pl.semaphore_wait(go_r, 1)
        second()
        for a in range(2):
            relay(a, 1)

    settle(0, 1)
    settle(1, 1)

    def turn(t, carry):
        m = lax.rem(t, 2)
        post = ((t < 2) & (s == 0)) | ((t >= 2) & (s > 0))

        @pl.when(((t == 0) & (s < half)) | ((t == 2) & (s >= half)))
        def _():
            values()

        @pl.when(t < 2)
        def _():
            chain_in(m)

        @pl.when(post)
        def _():
            post_in(m)

        @pl.when(t < 2)
        def _():
            chain_out(m)

        @pl.when(post)
        def _():
            post_out(m)

        return carry

    lax.fori_loop(0, 4, turn, 0)

    for m in range(2):
        for c in range(CHUNKS):
            sg[0, m, :, c * step:(c + 1) * step] = out[m, c].T
    for m in range(2):
        dq_copy(m).wait_recv()
        for c in range(CHUNKS):
            rows = slice(c * step, (c + 1) * step)
            dq[0, m, :, rows] = (dqown[m, rows] + dqrx[m, rows].astype(F32)).T.astype(BF16)


    @pl.when(cx == 0)
    def _():
        for j in range(1, SIDE):
            edge_out(j).wait_send()

    @pl.when(cx > 0)
    def _():
        for m in range(2):
            query_copy(m).wait_send()

    edge_over(False, False).wait_send()

    @pl.when(cx < SIDE - 1)
    def _():
        edge_in().wait_send()

    for m in range(2):
        dq_copy(m).wait_send()
        for side in range(2):
            stat_copy(m, side).wait_send()
            delta_copy(m, side).wait_send()
    for a in range(2):
        for d in range(1, SIDE):
            z_copy(a, d).wait_send()
        for h in range(2):
            for phase in range(2):
                for kind in range(4):
                    ring(a, h, phase, kind).wait_send()

    @pl.when(s < half)
    def _():
        mirror_copy().wait_send()

    @pl.when(odd)
    def _():
        for m in range(2):
            for c in range(CHUNKS):
                init_copy(m, c).wait_send()
                grad_copy(m, c, 1).wait_send()

    @pl.when(s > 0)
    def _():
        for m in range(2):
            for c in range(CHUNKS):
                grad_copy(m, c, 0).wait_send()

    @pl.when(s > half)
    def _():
        for m in range(2):
            skip_copy(m).wait_send()


def per_device(x_saved, queries, keys, value_weight, out_weight, out_grad):
    sections = lax.axis_size("section")
    blocks = lax.axis_size("seq")
    micro, rows, width = out_grad.shape
    shape = jax.ShapeDtypeStruct((1, micro, rows, width), BF16)
    step = width // CHUNKS
    vmem = pl.BlockSpec(memory_space=pltpu.VMEM)
    hbm = pl.BlockSpec(memory_space=pltpu.HBM)
    dma = pltpu.SemaphoreType.DMA
    block = pltpu.VMEM((micro, rows, width), BF16)
    turned = pltpu.VMEM((micro, width, rows), BF16)
    chunks = pltpu.VMEM((micro, CHUNKS, step, rows), BF16)
    side_rows = pltpu.VMEM((micro, 2, HEADS, rows), F32)
    return pl.pallas_call(
        functools.partial(kernel, sections, blocks, width),
        out_shape=(shape, shape, shape),
        in_specs=[hbm] * 6,
        out_specs=(vmem,) * 3,
        scratch_shapes=[
            pltpu.VMEM((2, SIDE, SIDE, SIDE, width // blocks, width), BF16),
            block,
            block,
            block,
            block,
            block,
            turned,
            block,
            block,
            block,
            pltpu.VMEM((micro, HEADS, rows, 2 * rows), F32),
            pltpu.VMEM((micro, HEADS, rows, 2 * rows), BF16),
            pltpu.VMEM((micro, 2, CHUNKS, step, rows), BF16),
            chunks,
            chunks,
            pltpu.VMEM((width, 2 * rows), F32),
            pltpu.VMEM((micro, width, 2 * rows), BF16),
            pltpu.VMEM((width, rows), BF16),
            pltpu.VMEM((micro, 2, 2, HEADS, rows), F32),
            pltpu.VMEM((micro, 2, 2, HEADS, rows), F32),
            pltpu.VMEM((2, HEADS, rows), F32),
            pltpu.VMEM((rows, 2 * rows), F32),
            pltpu.VMEM((HEADS, rows, 2 * rows), F32),
            side_rows,
            side_rows,
            pltpu.VMEM((micro, width, rows), F32),
            turned,
            turned,
            pltpu.VMEM((micro, rows // SIDE, width), BF16),
            pltpu.VMEM((micro, rows // SIDE, width), BF16),
            dma((6,)),
            dma((2,)), dma((2,)),
            dma((SIDE,)), dma((1,)),
            dma((1,)), dma((1,)),
            dma((1,)), dma((SIDE,)),
            dma((2, 2)), dma((2, 2)),
            dma((1,)), dma((1,)),
            dma((2, 3)), dma((2, 3)),
            dma((2, 2, 2, 4)), dma((2, 2, 2, 4)),
            dma((2, CHUNKS)),
            dma((2, 2, CHUNKS)), dma((2, 2, CHUNKS)),
            dma((2,)), dma((2,)),
            dma((2, 2)), dma((2, 2)),
            dma((2,)), dma((2,)),
            pltpu.SemaphoreType.REGULAR,
            pltpu.SemaphoreType.REGULAR,
        ],
        compiler_params=pltpu.CompilerParams(
            collective_id=0, has_side_effects=True, vmem_limit_bytes=60 * 2**20
        ),
        cost_estimate=pl.CostEstimate(flops=4 * 10**9, bytes_accessed=8 * 2**20, transcendentals=2**19),
        name="backward",
    )(x_saved, queries, keys, value_weight, out_weight, out_grad)


def solution(mesh):
    rows = P("section", None, "seq", None)
    weights = P("section", "seq", None)
    return jax.shard_map(
        per_device,
        mesh=mesh,
        in_specs=(rows, rows, rows, weights, weights, P(None, "seq", None)),
        out_specs=(rows, rows, rows),
        check_vma=False,
    )
```

```python
import functools
import math

import jax
import jax.numpy as jnp
from jax import lax
from jax.experimental import pallas as pl
from jax.experimental.pallas import tpu as pltpu
from jax.sharding import PartitionSpec as P

MESH = pl.DeviceIdType.MESH
HEADS = 8
HEAD = 128
ROWS = 128
SIDE = 4
CHUNKS = 4
BF16 = jnp.bfloat16
F32 = jnp.float32
NN = (((1,), (0,)), ((), ()))
NT = (((1,), (1,)), ((), ()))


def dot(left, right, dims=NN):
    return lax.dot_general(left, right, dims, preferred_element_type=F32)


def kernel(
    sections, blocks, width,
    x, q, k, wv, wo, og,
    sg, dq, dk,
    w, qv, kv, xv, ogv, qnext, kt, vals, xh, xmirror, weight, prob, grx, out, skip, acc, vgi, vg,
    stat, statrx, factor, bias, dprob, delta, deltarx, dqown, dqnext, dqrx, pass1, pass2, pass3, pass4,
    lsem, qsend, qrecv, e1send, e1recv, e2send, e2recv, e3send, e3recv, tsend, trecv, msend, mrecv, zsend, zrecv, rsend, rrecv, isend,
    gsend, grecv, ssend, srecv, esend, erecv, dsend, drecv, f1send, f1recv, f2send, f2recv, f3send, f3recv, go_z, go_r,
):
    s = lax.axis_index("section")
    i = lax.axis_index("seq")
    cy = lax.div(i, SIDE * SIDE)
    cz = lax.rem(lax.div(i, SIDE), SIDE)
    cx = lax.rem(i, SIDE)
    after = lax.rem(i + 1, blocks)
    before = lax.rem(i + blocks - 1, blocks)
    top = sections - 1
    half = sections // 2
    mirror_s = top - s
    step = width // CHUNKS
    scale = 1.0 / math.sqrt(HEAD)

    def at(y, z, x_):
        return y * (SIDE * SIDE) + z * SIDE + x_

    def copy(src, dst, send, recv, device):
        return pltpu.make_async_remote_copy(
            src_ref=src, dst_ref=dst, send_sem=send, recv_sem=recv,
            device_id=device, device_id_type=MESH,
        )


    def local_copy(n):
        src, dst = (
            (q.at[0], qv), (k.at[0], kv), (wo.at[0], w.at[0, cy, cz, cx]),
            (wv.at[0], w.at[1, cy, cz, cx]), (x.at[0], xv), (og, ogv),
        )[n]
        return pltpu.make_async_copy(src, dst, lsem.at[n])

    def query_copy(m):
        return copy(q.at[0, m], qnext.at[m], qsend.at[m], qrecv.at[m], (s, before))


    quarter = ROWS // SIDE
    back = lax.rem(i + blocks - SIDE, blocks)

    def edge_out(j):
        src = q.at[0, :, pl.ds(j * quarter, quarter)]
        return copy(src, pass1, e1send.at[j], e1recv.at[0], (s, i + j))

    def edge_over(first, last):
        src = q.at[0, :, pl.ds(0, quarter)] if first else pass1
        if last:
            dst, sem = qnext.at[:, pl.ds((SIDE - 1) * quarter, quarter)], e3recv.at[SIDE - 1]
        else:
            dst, sem = pass2, e2recv.at[0]
        return copy(src, dst, e2send.at[0], sem, (s, back))

    def edge_in():
        rows = pl.ds(pl.multiple_of(cx * quarter, quarter), quarter)
        to = i - cx + SIDE - 1
        return copy(pass2, qnext.at[:, rows], e3send.at[0], e3recv.at[cx], (s, to))

    def edge_arrival(j):
        part = qnext.at[:, pl.ds(j * quarter, quarter)]
        return copy(part, part, e3send.at[0], e3recv.at[j], (s, i))

    def stat_copy(m, side):
        to = before if side == 0 else after
        return copy(
            stat.at[m, side], statrx.at[m, 1 - side], tsend.at[m, side], trecv.at[m, 1 - side], (s, to)
        )

    def delta_copy(m, side):
        to = before if side == 0 else after
        return copy(
            delta.at[m, side], deltarx.at[m, 1 - side], esend.at[m, side], erecv.at[m, 1 - side], (s, to)
        )

    def mirror_copy():
        return copy(x.at[0], xmirror, msend.at[0], mrecv.at[0], (mirror_s, i))

    def z_copy(a, d):
        to = at(cy, lax.rem(cz + d, SIDE), cx)
        src = (wo if a == 0 else wv).at[0]
        return copy(src, w.at[a, cy, cz, cx], zsend.at[a, d - 1], zrecv.at[a, d - 1], (s, to))

    def z_arrival(a, d):
        piece = w.at[a, cy, lax.rem(cz + SIDE - d, SIDE), cx]
        return copy(piece, piece, zsend.at[a, d - 1], zrecv.at[a, d - 1], (s, i))

    def slab(a, h, phase, c, part):
        zs = pl.ds(2 * h, 2) if part is None else 2 * h + part
        if phase == 0:
            return w.at[a, cy, zs, c] if h == 0 else w.at[a, c, zs, cx]
        return w.at[a, c, zs] if h == 0 else w.at[a, :, zs, c]

    def kinds(h, phase):
        return (2,) if phase == h else (2, 3)

    def ring(a, h, phase, kind, arrival=False):
        along_x = phase == h
        me = cx if along_x else cy
        plus, minus = lax.rem(me + 1, SIDE), lax.rem(me + SIDE - 1, SIDE)
        across = lax.rem(me + 2, SIDE)
        part = None if kind < 2 or along_x else kind - 2
        if arrival:
            held = (minus, plus, across, across)[kind]
        else:
            held = (me, me, minus, plus)[kind]
        goes = plus if kind % 2 == 0 else minus
        to = at(cy, cz, goes) if along_x else at(goes, cz, cx)
        piece = slab(a, h, phase, held, part)
        sems = (a, h, phase, kind)
        return copy(piece, piece, rsend.at[sems], rrecv.at[sems], (s, to))

    def init_copy(m, c):
        return copy(
            grx.at[m, 0, c], grx.at[m, 1, c], isend.at[m, c], grecv.at[m, 1, c], (s, before)
        )

    def grad_copy(m, c, j):
        to = (s - 1, i) if j == 0 else (s - 1, before)
        return copy(out.at[m, c], grx.at[m, j, c], gsend.at[m, j, c], grecv.at[m, j, c], to)

    def skip_copy(m):
        return copy(out.at[m], skip.at[m], ssend.at[m], srecv.at[m], (mirror_s, i))

    def dq_copy(m):
        return copy(dqnext.at[m], dqrx.at[m], dsend.at[m], drecv.at[m], (s, after))


    ahead = lax.rem(i + SIDE, blocks)

    def dq_part(ref, m, j):
        return ref.at[m, pl.ds(j * step, step)]

    def dq_out(m, j):
        to = i - SIDE + 1 + j
        return copy(dq_part(dqnext, m, j), pass3.at[m], f1send.at[m, j], f1recv.at[m], (s, to))

    def dq_over(m, first, last):
        src = dq_part(dqnext, m, SIDE - 1) if first else pass3.at[m]
        if last:
            return copy(src, dq_part(dqrx, m, 0), f2send.at[m], f3recv.at[m, 0], (s, ahead))
        return copy(src, pass4.at[m], f2send.at[m], f2recv.at[m], (s, ahead))

    def dq_in(m):
        rows = pl.ds(pl.multiple_of(cx * step, step), step)
        return copy(pass4.at[m], dqrx.at[m, rows], f3send.at[m], f3recv.at[m, cx], (s, i - cx))

    def dq_arrival(m, j):
        part = dq_part(dqrx, m, j)
        return copy(part, part, f3send.at[m], f3recv.at[m, j], (s, i))

    for n in range(5):
        local_copy(n).start()

    @pl.when(s == top)
    def _():
        local_copy(5).start()


    barrier = pltpu.get_barrier_semaphore()

    def greet(section, seq):
        pl.semaphore_signal(barrier, inc=1, device_id=(section, seq), device_id_type=MESH)

    greet(s, after)
    greet(s, before)
    greet(mirror_s, i)
    for d in range(1, SIDE):
        greet(s, at(cy, lax.rem(cz + d, SIDE), cx))
        greet(s, at(cy, cz, lax.rem(cx + d, SIDE)))
    for d in (1, SIDE - 1):
        greet(s, at(lax.rem(cy + d, SIDE), cz, cx))
        greet(s, lax.rem(i + d * SIDE + (blocks - SIDE * SIDE if d > 1 else 0), blocks))

    @pl.when(s > 0)
    def _():
        greet(s - 1, i)
        greet(s - 1, before)

    @pl.when(s < top)
    def _():
        greet(s + 1, i)
        greet(s + 1, after)

    @pl.when(s > 1)
    def _():
        greet(s - 2, i)

    @pl.when(s < top - 1)
    def _():
        greet(s + 2, i)

    odd = lax.rem(s, 2) == 1
    peers = 13 + lax.div(s + 6, sections) + lax.div(2 * top - 1 - s, sections) + 2 * lax.div(s + top, sections) + 2 * lax.div(2 * top - s, sections)
    pl.semaphore_wait(barrier, peers)


    row = lax.broadcasted_iota(jnp.int32, (ROWS, 2 * ROWS), 0)
    col = lax.broadcasted_iota(jnp.int32, (ROWS, 2 * ROWS), 1)
    no_next = jnp.where(i == blocks - 1, 2 * ROWS, 0)
    allowed = ((col < ROWS) & (row <= col)) | ((col >= ROWS) & (row > col - ROWS + no_next))
    bias[...] = jnp.where(allowed, 0.0, -1e30)

    def each_head(body):
        for h in range(HEADS):
            body(h, slice(h * HEAD, (h + 1) * HEAD))

    def soft_in(m):
        @pl.when(cx < SIDE - 1)
        def _():
            query_copy(m).wait_recv()

        def head(h, cols):
            keys = kv[m, :, cols]
            queries = jnp.concatenate([qv[m, :, cols], qnext[m, :, cols]], 0)
            score = dot(keys, queries, NT) * scale + bias[...]
            high = jnp.maximum(jnp.max(score, axis=0, keepdims=True), -1e29)
            e = jnp.exp(score - high)
            total = jnp.sum(e, axis=0, keepdims=True)
            weight[m, h] = e
            one = slice(h, h + 1)
            stat[m, 0, 0, one] = high[:, :ROWS]
            stat[m, 1, 0, one] = high[:, ROWS:]
            stat[m, 0, 1, one] = total[:, :ROWS]
            stat[m, 1, 1, one] = total[:, ROWS:]
            kt[m, cols] = keys.T

        each_head(head)
        for side in range(2):
            stat_copy(m, side).start()

    def soft_out(m):
        for side in range(2):
            stat_copy(m, 1 - side).wait_recv()
            here, there = stat[m, side, 0], statrx[m, side, 0]
            high = jnp.maximum(here, there)
            mine = jnp.exp(here - high)
            total = stat[m, side, 1] * mine + statrx[m, side, 1] * jnp.exp(there - high)
            factor[side] = mine / total

        def head(h, cols):
            one = slice(h, h + 1)
            part = jnp.concatenate([factor[0, one], factor[1, one]], 1)
            prob[m, h] = (weight[m, h] * part).astype(BF16)

        each_head(head)

    def values():
        @pl.when(s >= half)
        def _():
            mirror_copy().wait_recv()
            xh[...] = (xv[...].astype(F32) + xmirror[...].astype(F32)).astype(BF16)

        @pl.when(s < half)
        def _():
            xh[...] = xv[...]

        def columns(c, carry):
            cols = pl.ds(pl.multiple_of(c * step, step), step)
            part = w[1, :, :, :, :, cols].reshape(width, step)
            result = dot(xh[...].reshape(2 * ROWS, width), part).astype(BF16)
            vals[:, :, cols] = result.reshape(2, ROWS, step)
            return carry

        lax.fori_loop(0, CHUNKS, columns, 0)

    def chain_in(m):
        acc[...] = jnp.zeros_like(acc)

        @pl.when((s < top) & (lax.rem(s, 2) == 0))
        def _():
            for c in range(CHUNKS):
                grad_copy(m, c, 0).wait_recv()

        @pl.when((s < top) & (lax.rem(s, 2) == 1))
        def _():
            for c in range(CHUNKS):
                grad_copy(m, c, 0).wait_recv()
                init_copy(m, c).start()

        def chunk(c, carry):
            grad_copy(m, c, 1).wait_recv()
            cols = pl.ds(pl.multiple_of(c * step, step), step)
            both = jnp.concatenate([grx[m, 0, c], grx[m, 1, c]], 1)
            part = w[0, :, :, :, :, cols].reshape(width, step)
            acc[...] += dot(part, both)
            return carry

        lax.fori_loop(0, CHUNKS, chunk, 0)
        vgi[m] = acc[...].astype(BF16)

    def chain_out(m):
        for h in range(HEADS):
            rows = slice(h * HEAD, (h + 1) * HEAD)
            vg[rows] = dot(vgi[m, rows], prob[m, h], NT).astype(BF16)

        @pl.when(s < half - 1)
        def _():
            skip_copy(m).wait_recv()

        @pl.when(s == half - 1)
        def _():
            skip[m] = grx[m, 0]

        def chunk(c, carry):
            part = w[1, c].reshape(step, width)
            total = dot(part, vg[...]) + grx[m, 0, c].astype(F32) + skip[m, c].astype(F32)
            out[m, c] = total.astype(BF16)

            @pl.when(lax.rem(s, 2) == 1)
            def _():
                grad_copy(m, c, 1).start()

            @pl.when(s > 0)
            def _():
                grad_copy(m, c, 0).start()

            return carry

        lax.fori_loop(0, CHUNKS, chunk, 0)

        @pl.when(s > half)
        def _():
            skip_copy(m).start()

    def post_in(m):
        def head(h, cols):
            grad = dot(vals[m, :, cols], vgi[m, cols])
            dprob[h] = grad
            total = jnp.sum(prob[m, h].astype(F32) * grad, axis=0, keepdims=True)
            one = slice(h, h + 1)
            delta[m, 0, one] = total[:, :ROWS]
            delta[m, 1, one] = total[:, ROWS:]

        each_head(head)
        for side in range(2):
            delta_copy(m, side).start()

    def post_out(m):
        for side in range(2):
            delta_copy(m, 1 - side).wait_recv()
            factor[side] = delta[m, side] + deltarx[m, side]

        def head(h, cols):
            one = slice(h, h + 1)
            whole = jnp.concatenate([factor[0, one], factor[1, one]], 1)
            ds = (prob[m, h].astype(F32) * (dprob[h] - whole) * scale).astype(BF16)
            queries = jnp.concatenate([qv[m, :, cols], qnext[m, :, cols]], 0)
            dk[0, m, :, cols] = dot(ds, queries).astype(BF16)
            both = dot(kt[m, cols], ds)
            dqown[m, cols] = both[:, :ROWS]
            dqnext[m, cols] = both[:, ROWS:].astype(BF16)

        each_head(head)

        @pl.when(cx < SIDE - 1)
        def _():
            dq_copy(m).start()

        @pl.when(cx == SIDE - 1)
        def _():
            for j in range(SIDE - 1):
                dq_out(m, j).start()
            dq_over(m, True, False).start()


    def relay(a, phase):
        for h in range(2):
            for kind in range(2):
                ring(a, h, phase, kind, True).wait_recv()
                if kind + 2 in kinds(h, phase):
                    ring(a, h, phase, kind + 2).start()

    def settle(a, phase):
        for h in range(2):
            for kind in kinds(h, phase):
                ring(a, h, phase, kind, True).wait_recv()

    def second():
        for a in range(2):
            settle(a, 0)
            for h in range(2):
                for kind in range(2):
                    ring(a, h, 1, kind).start()

    def each_micro(body):
        def turn(m, carry):
            body(m)
            return carry

        lax.fori_loop(0, 2, turn, 0)

    def start_queries():
        @pl.when(cx == 0)
        def _():
            for j in range(1, SIDE):
                edge_out(j).start()
            edge_over(True, False).start()

        @pl.when(cx > 0)
        def _():
            for m in range(2):
                query_copy(m).start()

    def edge_first():
        @pl.when(cx > 0)
        def _():
            edge_out(0).wait_recv()

        @pl.when((cx > 0) & (cx < SIDE - 1))
        def _():
            edge_over(False, False).start()

        @pl.when(cx == SIDE - 1)
        def _():
            edge_over(False, True).start()

    def edge_second():
        @pl.when(cx < SIDE - 1)
        def _():
            edge_over(False, False).wait_recv()
            edge_in().start()

    @pl.when(s < top - 1)
    def _():
        pl.semaphore_wait(go_z, 1)

    for a in range(2):
        for d in range(1, SIDE):
            z_copy(a, d).start()

    start_queries()

    for n in range(5):
        local_copy(n).wait()

    for a in range(2):
        for d in range(1, SIDE):
            z_arrival(a, d).wait_recv()
        for h in range(2):
            for kind in range(2):
                ring(a, h, 0, kind).start()

    @pl.when(s > 1)
    def _():
        pl.semaphore_signal(go_z, inc=1, device_id=(s - 2, i), device_id_type=MESH)

    @pl.when(s < half)
    def _():
        mirror_copy().start()

    edge_first()

    for a in range(2):
        relay(a, 0)

    edge_second()

    @pl.when(odd)
    def _():
        second()
        for a in range(2):
            relay(a, 1)
        pl.semaphore_signal(go_r, inc=1, device_id=(s - 1, i), device_id_type=MESH)

    @pl.when(s == top)
    def _():
        local_copy(5).wait()
        for m in range(2):
            for c in range(CHUNKS):
                grx[m, 0, c] = ogv[m, :, c * step:(c + 1) * step].T
                init_copy(m, c).start()

    @pl.when(s >= half)
    def _():
        skip[...] = jnp.zeros_like(skip)

    @pl.when(cx == SIDE - 1)
    def _():
        for j in range(SIDE):
            edge_arrival(j).wait_recv()

    each_micro(soft_in)

    each_micro(soft_out)

    @pl.when(jnp.logical_not(odd))
    def _():
        pl.semaphore_wait(go_r, 1)
        second()
        for a in range(2):
            relay(a, 1)

    settle(0, 1)
    settle(1, 1)

    def turn(t, carry):
        m = lax.rem(t, 2)
        post = ((t < 2) & (s == 0)) | ((t >= 2) & (s > 0))

        @pl.when(((t == 0) & (s < half)) | ((t == 2) & (s >= half)))
        def _():
            values()

        @pl.when(t < 2)
        def _():
            chain_in(m)

        @pl.when(post)
        def _():
            post_in(m)

        @pl.when(t < 2)
        def _():
            chain_out(m)

        @pl.when(post)
        def _():
            post_out(m)

        return carry

    lax.fori_loop(0, 4, turn, 0)

    for m in range(2):
        @pl.when(cx < SIDE - 1)
        def _():
            dq_out(m, 0).wait_recv()

        @pl.when((cx > 0) & (cx < SIDE - 1))
        def _():
            dq_over(m, False, False).start()

        @pl.when(cx == 0)
        def _():
            dq_over(m, False, True).start()

    for m in range(2):
        @pl.when(cx > 0)
        def _():
            dq_over(m, False, False).wait_recv()
            dq_in(m).start()

    for m in range(2):
        for c in range(CHUNKS):
            sg[0, m, :, c * step:(c + 1) * step] = out[m, c].T
    for m in range(2):
        @pl.when(cx > 0)
        def _():
            dq_copy(m).wait_recv()

        @pl.when(cx == 0)
        def _():
            for j in range(SIDE):
                dq_arrival(m, j).wait_recv()

        for c in range(CHUNKS):
            rows = slice(c * step, (c + 1) * step)
            dq[0, m, :, rows] = (dqown[m, rows] + dqrx[m, rows].astype(F32)).T.astype(BF16)


    @pl.when(cx == 0)
    def _():
        for j in range(1, SIDE):
            edge_out(j).wait_send()

    @pl.when(cx > 0)
    def _():
        for m in range(2):
            query_copy(m).wait_send()

    edge_over(False, False).wait_send()

    @pl.when(cx < SIDE - 1)
    def _():
        edge_in().wait_send()

    for m in range(2):
        @pl.when(cx < SIDE - 1)
        def _():
            dq_copy(m).wait_send()

        @pl.when(cx == SIDE - 1)
        def _():
            for j in range(SIDE - 1):
                dq_out(m, j).wait_send()

        dq_over(m, False, False).wait_send()

        @pl.when(cx > 0)
        def _():
            dq_in(m).wait_send()

        for side in range(2):
            stat_copy(m, side).wait_send()
            delta_copy(m, side).wait_send()
    for a in range(2):
        for d in range(1, SIDE):
            z_copy(a, d).wait_send()
        for h in range(2):
            for phase in range(2):
                for kind in (0, 1) + kinds(h, phase):
                    ring(a, h, phase, kind).wait_send()

    @pl.when(s < half)
    def _():
        mirror_copy().wait_send()

    @pl.when(odd)
    def _():
        for m in range(2):
            for c in range(CHUNKS):
                init_copy(m, c).wait_send()
                grad_copy(m, c, 1).wait_send()

    @pl.when(s > 0)
    def _():
        for m in range(2):
            for c in range(CHUNKS):
                grad_copy(m, c, 0).wait_send()

    @pl.when(s > half)
    def _():
        for m in range(2):
            skip_copy(m).wait_send()


def per_device(x_saved, queries, keys, value_weight, out_weight, out_grad):
    sections = lax.axis_size("section")
    blocks = lax.axis_size("seq")
    micro, rows, width = out_grad.shape
    shape = jax.ShapeDtypeStruct((1, micro, rows, width), BF16)
    step = width // CHUNKS
    vmem = pl.BlockSpec(memory_space=pltpu.VMEM)
    hbm = pl.BlockSpec(memory_space=pltpu.HBM)
    dma = pltpu.SemaphoreType.DMA
    block = pltpu.VMEM((micro, rows, width), BF16)
    turned = pltpu.VMEM((micro, width, rows), BF16)
    chunks = pltpu.VMEM((micro, CHUNKS, step, rows), BF16)
    side_rows = pltpu.VMEM((micro, 2, HEADS, rows), F32)
    return pl.pallas_call(
        functools.partial(kernel, sections, blocks, width),
        out_shape=(shape, shape, shape),
        in_specs=[hbm] * 6,
        out_specs=(vmem,) * 3,
        scratch_shapes=[
            pltpu.VMEM((2, SIDE, SIDE, SIDE, width // blocks, width), BF16),
            block,
            block,
            block,
            block,
            block,
            turned,
            block,
            block,
            block,
            pltpu.VMEM((micro, HEADS, rows, 2 * rows), F32),
            pltpu.VMEM((micro, HEADS, rows, 2 * rows), BF16),
            pltpu.VMEM((micro, 2, CHUNKS, step, rows), BF16),
            chunks,
            chunks,
            pltpu.VMEM((width, 2 * rows), F32),
            pltpu.VMEM((micro, width, 2 * rows), BF16),
            pltpu.VMEM((width, rows), BF16),
            pltpu.VMEM((micro, 2, 2, HEADS, rows), F32),
            pltpu.VMEM((micro, 2, 2, HEADS, rows), F32),
            pltpu.VMEM((2, HEADS, rows), F32),
            pltpu.VMEM((rows, 2 * rows), F32),
            pltpu.VMEM((HEADS, rows, 2 * rows), F32),
            side_rows,
            side_rows,
            pltpu.VMEM((micro, width, rows), F32),
            turned,
            turned,
            pltpu.VMEM((micro, rows // SIDE, width), BF16),
            pltpu.VMEM((micro, rows // SIDE, width), BF16),
            pltpu.VMEM((micro, step, rows), BF16),
            pltpu.VMEM((micro, step, rows), BF16),
            dma((6,)),
            dma((2,)), dma((2,)),
            dma((SIDE,)), dma((1,)),
            dma((1,)), dma((1,)),
            dma((1,)), dma((SIDE,)),
            dma((2, 2)), dma((2, 2)),
            dma((1,)), dma((1,)),
            dma((2, 3)), dma((2, 3)),
            dma((2, 2, 2, 4)), dma((2, 2, 2, 4)),
            dma((2, CHUNKS)),
            dma((2, 2, CHUNKS)), dma((2, 2, CHUNKS)),
            dma((2,)), dma((2,)),
            dma((2, 2)), dma((2, 2)),
            dma((2,)), dma((2,)),
            dma((2, SIDE)), dma((2,)),
            dma((2,)), dma((2,)),
            dma((2,)), dma((2, SIDE)),
            pltpu.SemaphoreType.REGULAR,
            pltpu.SemaphoreType.REGULAR,
        ],
        compiler_params=pltpu.CompilerParams(
            collective_id=0, has_side_effects=True, vmem_limit_bytes=60 * 2**20
        ),
        cost_estimate=pl.CostEstimate(flops=4 * 10**9, bytes_accessed=8 * 2**20, transcendentals=2**19),
        name="backward",
    )(x_saved, queries, keys, value_weight, out_weight, out_grad)


def solution(mesh):
    rows = P("section", None, "seq", None)
    weights = P("section", "seq", None)
    return jax.shard_map(
        per_device,
        mesh=mesh,
        in_specs=(rows, rows, rows, weights, weights, P(None, "seq", None)),
        out_specs=(rows, rows, rows),
        check_vma=False,
    )
```

```python
import functools
import math

import jax
import jax.numpy as jnp
from jax import lax
from jax.experimental import pallas as pl
from jax.experimental.pallas import tpu as pltpu
from jax.sharding import PartitionSpec as P

MESH = pl.DeviceIdType.MESH
HEADS = 8
HEAD = 128
ROWS = 128
SIDE = 4
CHUNKS = 2
BF16 = jnp.bfloat16
F32 = jnp.float32
NN = (((1,), (0,)), ((), ()))
NT = (((1,), (1,)), ((), ()))


def dot(left, right, dims=NN):
    return lax.dot_general(left, right, dims, preferred_element_type=F32)


def kernel(
    sections, blocks, width,
    x, q, k, wv, wo, og,
    sg, dq, dk,
    w, qv, kv, xv, ogv, qnext, kt, vals, xh, xmirror, weight, prob, grx, out, skip, acc, vgi, vg,
    stat, statrx, factor, bias, dprob, delta, deltarx, dqown, dqnext, dqrx, pass1, pass2, pass3, pass4,
    lsem, qsend, qrecv, e1send, e1recv, e2send, e2recv, e3send, e3recv, tsend, trecv, msend, mrecv, zsend, zrecv, rsend, rrecv, isend,
    gsend, grecv, ssend, srecv, esend, erecv, dsend, drecv, f1send, f1recv, f2send, f2recv, f3send, f3recv, go_z, go_r,
):
    s = lax.axis_index("section")
    i = lax.axis_index("seq")
    cy = lax.div(i, SIDE * SIDE)
    cz = lax.rem(lax.div(i, SIDE), SIDE)
    cx = lax.rem(i, SIDE)
    after = lax.rem(i + 1, blocks)
    before = lax.rem(i + blocks - 1, blocks)
    top = sections - 1
    half = sections // 2
    mirror_s = top - s
    step = width // CHUNKS
    scale = 1.0 / math.sqrt(HEAD)

    def at(y, z, x_):
        return y * (SIDE * SIDE) + z * SIDE + x_

    def copy(src, dst, send, recv, device):
        return pltpu.make_async_remote_copy(
            src_ref=src, dst_ref=dst, send_sem=send, recv_sem=recv,
            device_id=device, device_id_type=MESH,
        )


    def local_copy(n):
        src, dst = (
            (q.at[0], qv), (k.at[0], kv), (wo.at[0], w.at[0, cy, cz, cx]),
            (wv.at[0], w.at[1, cy, cz, cx]), (x.at[0], xv), (og, ogv),
        )[n]
        return pltpu.make_async_copy(src, dst, lsem.at[n])

    def query_copy(m):
        return copy(q.at[0, m], qnext.at[m], qsend.at[m], qrecv.at[m], (s, before))


    quarter = ROWS // SIDE
    back = lax.rem(i + blocks - SIDE, blocks)

    def edge_out(j):
        src = q.at[0, :, pl.ds(j * quarter, quarter)]
        return copy(src, pass1, e1send.at[j], e1recv.at[0], (s, i + j))

    def edge_over(first, last):
        src = q.at[0, :, pl.ds(0, quarter)] if first else pass1
        if last:
            dst, sem = qnext.at[:, pl.ds((SIDE - 1) * quarter, quarter)], e3recv.at[SIDE - 1]
        else:
            dst, sem = pass2, e2recv.at[0]
        return copy(src, dst, e2send.at[0], sem, (s, back))

    def edge_in():
        rows = pl.ds(pl.multiple_of(cx * quarter, quarter), quarter)
        to = i - cx + SIDE - 1
        return copy(pass2, qnext.at[:, rows], e3send.at[0], e3recv.at[cx], (s, to))

    def edge_arrival(j):
        part = qnext.at[:, pl.ds(j * quarter, quarter)]
        return copy(part, part, e3send.at[0], e3recv.at[j], (s, i))

    def stat_copy(m, side):
        to = before if side == 0 else after
        return copy(
            stat.at[m, side], statrx.at[m, 1 - side], tsend.at[m, side], trecv.at[m, 1 - side], (s, to)
        )

    def delta_copy(m, side):
        to = before if side == 0 else after
        return copy(
            delta.at[m, side], deltarx.at[m, 1 - side], esend.at[m, side], erecv.at[m, 1 - side], (s, to)
        )

    def mirror_copy():
        return copy(x.at[0], xmirror, msend.at[0], mrecv.at[0], (mirror_s, i))

    def z_copy(a, d):
        to = at(cy, lax.rem(cz + d, SIDE), cx)
        src = (wo if a == 0 else wv).at[0]
        return copy(src, w.at[a, cy, cz, cx], zsend.at[a, d - 1], zrecv.at[a, d - 1], (s, to))

    def z_arrival(a, d):
        piece = w.at[a, cy, lax.rem(cz + SIDE - d, SIDE), cx]
        return copy(piece, piece, zsend.at[a, d - 1], zrecv.at[a, d - 1], (s, i))

    def slab(a, h, phase, c, part):
        zs = pl.ds(2 * h, 2) if part is None else 2 * h + part
        if phase == 0:
            return w.at[a, cy, zs, c] if h == 0 else w.at[a, c, zs, cx]
        return w.at[a, c, zs] if h == 0 else w.at[a, :, zs, c]

    def kinds(h, phase):
        return (2,) if phase == h else (2, 3)

    def ring(a, h, phase, kind, arrival=False):
        along_x = phase == h
        me = cx if along_x else cy
        plus, minus = lax.rem(me + 1, SIDE), lax.rem(me + SIDE - 1, SIDE)
        across = lax.rem(me + 2, SIDE)
        part = None if kind < 2 or along_x else kind - 2
        if arrival:
            held = (minus, plus, across, across)[kind]
        else:
            held = (me, me, minus, plus)[kind]
        goes = plus if kind % 2 == 0 else minus
        to = at(cy, cz, goes) if along_x else at(goes, cz, cx)
        piece = slab(a, h, phase, held, part)
        sems = (a, h, phase, kind)
        return copy(piece, piece, rsend.at[sems], rrecv.at[sems], (s, to))

    def init_copy(m, c):
        return copy(
            grx.at[m, 0, c], grx.at[m, 1, c], isend.at[m, c], grecv.at[m, 1, c], (s, before)
        )

    def grad_copy(m, c, j):
        to = (s - 1, i) if j == 0 else (s - 1, before)
        return copy(out.at[m, c], grx.at[m, j, c], gsend.at[m, j, c], grecv.at[m, j, c], to)

    def skip_copy(m):
        return copy(out.at[m], skip.at[m], ssend.at[m], srecv.at[m], (mirror_s, i))

    def dq_copy(m):
        return copy(dqnext.at[m], dqrx.at[m], dsend.at[m], drecv.at[m], (s, after))


    ahead = lax.rem(i + SIDE, blocks)
    fourth = width // SIDE

    def dq_part(ref, m, j):
        return ref.at[m, pl.ds(j * fourth, fourth)]

    def dq_out(m, j):
        to = i - SIDE + 1 + j
        return copy(dq_part(dqnext, m, j), pass3.at[m], f1send.at[m, j], f1recv.at[m], (s, to))

    def dq_over(m, first, last):
        src = dq_part(dqnext, m, SIDE - 1) if first else pass3.at[m]
        if last:
            return copy(src, dq_part(dqrx, m, 0), f2send.at[m], f3recv.at[m, 0], (s, ahead))
        return copy(src, pass4.at[m], f2send.at[m], f2recv.at[m], (s, ahead))

    def dq_in(m):
        rows = pl.ds(pl.multiple_of(cx * fourth, fourth), fourth)
        return copy(pass4.at[m], dqrx.at[m, rows], f3send.at[m], f3recv.at[m, cx], (s, i - cx))

    def dq_arrival(m, j):
        part = dq_part(dqrx, m, j)
        return copy(part, part, f3send.at[m], f3recv.at[m, j], (s, i))

    for n in range(5):
        local_copy(n).start()

    @pl.when(s == top)
    def _():
        local_copy(5).start()


    barrier = pltpu.get_barrier_semaphore()

    def greet(section, seq):
        pl.semaphore_signal(barrier, inc=1, device_id=(section, seq), device_id_type=MESH)

    greet(s, after)
    greet(s, before)
    greet(mirror_s, i)
    for d in range(1, SIDE):
        greet(s, at(cy, lax.rem(cz + d, SIDE), cx))
        greet(s, at(cy, cz, lax.rem(cx + d, SIDE)))
    for d in (1, SIDE - 1):
        greet(s, at(lax.rem(cy + d, SIDE), cz, cx))
        greet(s, lax.rem(i + d * SIDE + (blocks - SIDE * SIDE if d > 1 else 0), blocks))

    @pl.when(s > 0)
    def _():
        greet(s - 1, i)
        greet(s - 1, before)

    @pl.when(s < top)
    def _():
        greet(s + 1, i)
        greet(s + 1, after)

    @pl.when(s > 1)
    def _():
        greet(s - 2, i)

    @pl.when(s < top - 1)
    def _():
        greet(s + 2, i)

    odd = lax.rem(s, 2) == 1
    peers = 13 + lax.div(s + 6, sections) + lax.div(2 * top - 1 - s, sections) + 2 * lax.div(s + top, sections) + 2 * lax.div(2 * top - s, sections)
    pl.semaphore_wait(barrier, peers)


    row = lax.broadcasted_iota(jnp.int32, (ROWS, 2 * ROWS), 0)
    col = lax.broadcasted_iota(jnp.int32, (ROWS, 2 * ROWS), 1)
    no_next = jnp.where(i == blocks - 1, 2 * ROWS, 0)
    allowed = ((col < ROWS) & (row <= col)) | ((col >= ROWS) & (row > col - ROWS + no_next))
    bias[...] = jnp.where(allowed, 0.0, -1e30)

    def each_head(body):
        for h in range(HEADS):
            body(h, slice(h * HEAD, (h + 1) * HEAD))

    def soft_in(m):
        @pl.when(cx < SIDE - 1)
        def _():
            query_copy(m).wait_recv()

        def head(h, cols):
            keys = kv[m, :, cols]
            queries = jnp.concatenate([qv[m, :, cols], qnext[m, :, cols]], 0)
            score = dot(keys, queries, NT) * scale + bias[...]
            high = jnp.maximum(jnp.max(score, axis=0, keepdims=True), -1e29)
            e = jnp.exp(score - high)
            total = jnp.sum(e, axis=0, keepdims=True)
            weight[m, h] = e
            one = slice(h, h + 1)
            stat[m, 0, 0, one] = high[:, :ROWS]
            stat[m, 1, 0, one] = high[:, ROWS:]
            stat[m, 0, 1, one] = total[:, :ROWS]
            stat[m, 1, 1, one] = total[:, ROWS:]
            kt[m, cols] = keys.T

        each_head(head)
        for side in range(2):
            stat_copy(m, side).start()

    def soft_out(m):
        for side in range(2):
            stat_copy(m, 1 - side).wait_recv()
            here, there = stat[m, side, 0], statrx[m, side, 0]
            high = jnp.maximum(here, there)
            mine = jnp.exp(here - high)
            total = stat[m, side, 1] * mine + statrx[m, side, 1] * jnp.exp(there - high)
            factor[side] = mine / total

        def head(h, cols):
            one = slice(h, h + 1)
            part = jnp.concatenate([factor[0, one], factor[1, one]], 1)
            prob[m, h] = (weight[m, h] * part).astype(BF16)

        each_head(head)

    def values():
        @pl.when(s >= half)
        def _():
            mirror_copy().wait_recv()
            xh[...] = (xv[...].astype(F32) + xmirror[...].astype(F32)).astype(BF16)

        @pl.when(s < half)
        def _():
            xh[...] = xv[...]

        def columns(c, carry):
            cols = pl.ds(pl.multiple_of(c * step, step), step)
            part = w[1, :, :, :, :, cols].reshape(width, step)
            result = dot(xh[...].reshape(2 * ROWS, width), part).astype(BF16)
            vals[:, :, cols] = result.reshape(2, ROWS, step)
            return carry

        lax.fori_loop(0, CHUNKS, columns, 0)

    def chain_in(m):
        acc[...] = jnp.zeros_like(acc)

        @pl.when((s < top) & (lax.rem(s, 2) == 0))
        def _():
            for c in range(CHUNKS):
                grad_copy(m, c, 0).wait_recv()

        @pl.when((s < top) & (lax.rem(s, 2) == 1))
        def _():
            for c in range(CHUNKS):
                grad_copy(m, c, 0).wait_recv()
                init_copy(m, c).start()

        def chunk(c, carry):
            grad_copy(m, c, 1).wait_recv()
            cols = pl.ds(pl.multiple_of(c * step, step), step)
            both = jnp.concatenate([grx[m, 0, c], grx[m, 1, c]], 1)
            part = w[0, :, :, :, :, cols].reshape(width, step)
            acc[...] += dot(part, both)
            return carry

        lax.fori_loop(0, CHUNKS, chunk, 0)
        vgi[m] = acc[...].astype(BF16)

    def chain_out(m):
        for h in range(HEADS):
            rows = slice(h * HEAD, (h + 1) * HEAD)
            vg[rows] = dot(vgi[m, rows], prob[m, h], NT).astype(BF16)

        @pl.when(s < half - 1)
        def _():
            skip_copy(m).wait_recv()

        @pl.when(s == half - 1)
        def _():
            skip[m] = grx[m, 0]

        def chunk(c, carry):
            part = w[1, pl.ds(c * (SIDE // CHUNKS), SIDE // CHUNKS)].reshape(step, width)
            total = dot(part, vg[...]) + grx[m, 0, c].astype(F32) + skip[m, c].astype(F32)
            out[m, c] = total.astype(BF16)

            @pl.when(lax.rem(s, 2) == 1)
            def _():
                grad_copy(m, c, 1).start()

            @pl.when(s > 0)
            def _():
                grad_copy(m, c, 0).start()

            return carry

        lax.fori_loop(0, CHUNKS, chunk, 0)

        @pl.when(s > half)
        def _():
            skip_copy(m).start()

    def post_in(m):
        def head(h, cols):
            grad = dot(vals[m, :, cols], vgi[m, cols])
            dprob[h] = grad
            total = jnp.sum(prob[m, h].astype(F32) * grad, axis=0, keepdims=True)
            one = slice(h, h + 1)
            delta[m, 0, one] = total[:, :ROWS]
            delta[m, 1, one] = total[:, ROWS:]

        each_head(head)
        for side in range(2):
            delta_copy(m, side).start()

    def post_out(m):
        for side in range(2):
            delta_copy(m, 1 - side).wait_recv()
            factor[side] = delta[m, side] + deltarx[m, side]

        def head(h, cols):
            one = slice(h, h + 1)
            whole = jnp.concatenate([factor[0, one], factor[1, one]], 1)
            ds = (prob[m, h].astype(F32) * (dprob[h] - whole) * scale).astype(BF16)
            queries = jnp.concatenate([qv[m, :, cols], qnext[m, :, cols]], 0)
            dk[0, m, :, cols] = dot(ds, queries).astype(BF16)
            both = dot(kt[m, cols], ds)
            dqown[m, cols] = both[:, :ROWS]
            dqnext[m, cols] = both[:, ROWS:].astype(BF16)

        each_head(head)

        @pl.when(cx < SIDE - 1)
        def _():
            dq_copy(m).start()

        @pl.when(cx == SIDE - 1)
        def _():
            for j in range(SIDE - 1):
                dq_out(m, j).start()
            dq_over(m, True, False).start()


    def relay(a, phase):
        for h in range(2):
            for kind in range(2):
                ring(a, h, phase, kind, True).wait_recv()
                if kind + 2 in kinds(h, phase):
                    ring(a, h, phase, kind + 2).start()

    def settle(a, phase):
        for h in range(2):
            for kind in kinds(h, phase):
                ring(a, h, phase, kind, True).wait_recv()

    def second():
        for a in range(2):
            settle(a, 0)
            for h in range(2):
                for kind in range(2):
                    ring(a, h, 1, kind).start()

    def each_micro(body):
        def turn(m, carry):
            body(m)
            return carry

        lax.fori_loop(0, 2, turn, 0)

    def start_queries():
        @pl.when(cx == 0)
        def _():
            for j in range(1, SIDE):
                edge_out(j).start()
            edge_over(True, False).start()

        @pl.when(cx > 0)
        def _():
            for m in range(2):
                query_copy(m).start()

    def edge_first():
        @pl.when(cx > 0)
        def _():
            edge_out(0).wait_recv()

        @pl.when((cx > 0) & (cx < SIDE - 1))
        def _():
            edge_over(False, False).start()

        @pl.when(cx == SIDE - 1)
        def _():
            edge_over(False, True).start()

    def edge_second():
        @pl.when(cx < SIDE - 1)
        def _():
            edge_over(False, False).wait_recv()
            edge_in().start()

    @pl.when(s < top - 1)
    def _():
        pl.semaphore_wait(go_z, 1)

    for a in range(2):
        for d in range(1, SIDE):
            z_copy(a, d).start()

    start_queries()

    for n in range(5):
        local_copy(n).wait()

    for a in range(2):
        for d in range(1, SIDE):
            z_arrival(a, d).wait_recv()
        for h in range(2):
            for kind in range(2):
                ring(a, h, 0, kind).start()

    @pl.when(s > 1)
    def _():
        pl.semaphore_signal(go_z, inc=1, device_id=(s - 2, i), device_id_type=MESH)

    edge_first()

    for a in range(2):
        relay(a, 0)

    edge_second()

    @pl.when(odd)
    def _():
        second()
        for a in range(2):
            relay(a, 1)
        pl.semaphore_signal(go_r, inc=1, device_id=(s - 1, i), device_id_type=MESH)

    @pl.when(s == top)
    def _():
        local_copy(5).wait()
        for m in range(2):
            for c in range(CHUNKS):
                grx[m, 0, c] = ogv[m, :, c * step:(c + 1) * step].T
                init_copy(m, c).start()

    @pl.when(s >= half)
    def _():
        skip[...] = jnp.zeros_like(skip)

    @pl.when(cx == SIDE - 1)
    def _():
        for j in range(SIDE):
            edge_arrival(j).wait_recv()

    each_micro(soft_in)

    each_micro(soft_out)

    @pl.when(jnp.logical_not(odd))
    def _():
        pl.semaphore_wait(go_r, 1)
        second()
        for a in range(2):
            relay(a, 1)

    settle(0, 1)
    settle(1, 1)

    @pl.when(s < half)
    def _():
        mirror_copy().start()

    def turn(t, carry):
        m = lax.rem(t, 2)
        post = ((t < 2) & (s == 0)) | ((t >= 2) & (s > 0))

        @pl.when(((t == 0) & (s < half)) | ((t == 2) & (s >= half)))
        def _():
            values()

        @pl.when(t < 2)
        def _():
            chain_in(m)

        @pl.when(post)
        def _():
            post_in(m)

        @pl.when(t < 2)
        def _():
            chain_out(m)

        @pl.when(post)
        def _():
            post_out(m)

        return carry

    lax.fori_loop(0, 4, turn, 0)

    for m in range(2):
        @pl.when(cx < SIDE - 1)
        def _():
            dq_out(m, 0).wait_recv()

        @pl.when((cx > 0) & (cx < SIDE - 1))
        def _():
            dq_over(m, False, False).start()

        @pl.when(cx == 0)
        def _():
            dq_over(m, False, True).start()

    for m in range(2):
        @pl.when(cx > 0)
        def _():
            dq_over(m, False, False).wait_recv()
            dq_in(m).start()

    for m in range(2):
        for c in range(CHUNKS):
            sg[0, m, :, c * step:(c + 1) * step] = out[m, c].T
    for m in range(2):
        @pl.when(cx > 0)
        def _():
            dq_copy(m).wait_recv()

        @pl.when(cx == 0)
        def _():
            for j in range(SIDE):
                dq_arrival(m, j).wait_recv()

        for c in range(CHUNKS):
            rows = slice(c * step, (c + 1) * step)
            dq[0, m, :, rows] = (dqown[m, rows] + dqrx[m, rows].astype(F32)).T.astype(BF16)


    @pl.when(cx == 0)
    def _():
        for j in range(1, SIDE):
            edge_out(j).wait_send()

    @pl.when(cx > 0)
    def _():
        for m in range(2):
            query_copy(m).wait_send()

    edge_over(False, False).wait_send()

    @pl.when(cx < SIDE - 1)
    def _():
        edge_in().wait_send()

    for m in range(2):
        @pl.when(cx < SIDE - 1)
        def _():
            dq_copy(m).wait_send()

        @pl.when(cx == SIDE - 1)
        def _():
            for j in range(SIDE - 1):
                dq_out(m, j).wait_send()

        dq_over(m, False, False).wait_send()

        @pl.when(cx > 0)
        def _():
            dq_in(m).wait_send()

        for side in range(2):
            stat_copy(m, side).wait_send()
            delta_copy(m, side).wait_send()
    for a in range(2):
        for d in range(1, SIDE):
            z_copy(a, d).wait_send()
        for h in range(2):
            for phase in range(2):
                for kind in (0, 1) + kinds(h, phase):
                    ring(a, h, phase, kind).wait_send()

    @pl.when(s < half)
    def _():
        mirror_copy().wait_send()

    @pl.when(odd)
    def _():
        for m in range(2):
            for c in range(CHUNKS):
                init_copy(m, c).wait_send()
                grad_copy(m, c, 1).wait_send()

    @pl.when(s > 0)
    def _():
        for m in range(2):
            for c in range(CHUNKS):
                grad_copy(m, c, 0).wait_send()

    @pl.when(s > half)
    def _():
        for m in range(2):
            skip_copy(m).wait_send()


def per_device(x_saved, queries, keys, value_weight, out_weight, out_grad):
    sections = lax.axis_size("section")
    blocks = lax.axis_size("seq")
    micro, rows, width = out_grad.shape
    shape = jax.ShapeDtypeStruct((1, micro, rows, width), BF16)
    step = width // CHUNKS
    vmem = pl.BlockSpec(memory_space=pltpu.VMEM)
    hbm = pl.BlockSpec(memory_space=pltpu.HBM)
    dma = pltpu.SemaphoreType.DMA
    block = pltpu.VMEM((micro, rows, width), BF16)
    turned = pltpu.VMEM((micro, width, rows), BF16)
    chunks = pltpu.VMEM((micro, CHUNKS, step, rows), BF16)
    side_rows = pltpu.VMEM((micro, 2, HEADS, rows), F32)
    return pl.pallas_call(
        functools.partial(kernel, sections, blocks, width),
        out_shape=(shape, shape, shape),
        in_specs=[hbm] * 6,
        out_specs=(vmem,) * 3,
        scratch_shapes=[
            pltpu.VMEM((2, SIDE, SIDE, SIDE, width // blocks, width), BF16),
            block,
            block,
            block,
            block,
            block,
            turned,
            block,
            block,
            block,
            pltpu.VMEM((micro, HEADS, rows, 2 * rows), F32),
            pltpu.VMEM((micro, HEADS, rows, 2 * rows), BF16),
            pltpu.VMEM((micro, 2, CHUNKS, step, rows), BF16),
            chunks,
            chunks,
            pltpu.VMEM((width, 2 * rows), F32),
            pltpu.VMEM((micro, width, 2 * rows), BF16),
            pltpu.VMEM((width, rows), BF16),
            pltpu.VMEM((micro, 2, 2, HEADS, rows), F32),
            pltpu.VMEM((micro, 2, 2, HEADS, rows), F32),
            pltpu.VMEM((2, HEADS, rows), F32),
            pltpu.VMEM((rows, 2 * rows), F32),
            pltpu.VMEM((HEADS, rows, 2 * rows), F32),
            side_rows,
            side_rows,
            pltpu.VMEM((micro, width, rows), F32),
            turned,
            turned,
            pltpu.VMEM((micro, rows // SIDE, width), BF16),
            pltpu.VMEM((micro, rows // SIDE, width), BF16),
            pltpu.VMEM((micro, width // SIDE, rows), BF16),
            pltpu.VMEM((micro, width // SIDE, rows), BF16),
            dma((6,)),
            dma((2,)), dma((2,)),
            dma((SIDE,)), dma((1,)),
            dma((1,)), dma((1,)),
            dma((1,)), dma((SIDE,)),
            dma((2, 2)), dma((2, 2)),
            dma((1,)), dma((1,)),
            dma((2, 3)), dma((2, 3)),
            dma((2, 2, 2, 4)), dma((2, 2, 2, 4)),
            dma((2, CHUNKS)),
            dma((2, 2, CHUNKS)), dma((2, 2, CHUNKS)),
            dma((2,)), dma((2,)),
            dma((2, 2)), dma((2, 2)),
            dma((2,)), dma((2,)),
            dma((2, SIDE)), dma((2,)),
            dma((2,)), dma((2,)),
            dma((2,)), dma((2, SIDE)),
            pltpu.SemaphoreType.REGULAR,
            pltpu.SemaphoreType.REGULAR,
        ],
        compiler_params=pltpu.CompilerParams(
            collective_id=0, has_side_effects=True, vmem_limit_bytes=60 * 2**20
        ),
        cost_estimate=pl.CostEstimate(flops=4 * 10**9, bytes_accessed=8 * 2**20, transcendentals=2**19),
        name="backward",
    )(x_saved, queries, keys, value_weight, out_weight, out_grad)


def solution(mesh):
    rows = P("section", None, "seq", None)
    weights = P("section", "seq", None)
    return jax.shard_map(
        per_device,
        mesh=mesh,
        in_specs=(rows, rows, rows, weights, weights, P(None, "seq", None)),
        out_specs=(rows, rows, rows),
        check_vma=False,
    )
```

```python
import functools
import math

import jax
import jax.numpy as jnp
from jax import lax
from jax.experimental import pallas as pl
from jax.experimental.pallas import tpu as pltpu
from jax.sharding import PartitionSpec as P

MESH = pl.DeviceIdType.MESH
HEADS = 8
HEAD = 128
ROWS = 128
SIDE = 4
CHUNKS = 4
BF16 = jnp.bfloat16
F32 = jnp.float32
NN = (((1,), (0,)), ((), ()))
NT = (((1,), (1,)), ((), ()))


def dot(left, right, dims=NN):
    return lax.dot_general(left, right, dims, preferred_element_type=F32)


def kernel(
    sections, blocks, width,
    x, q, k, wv, wo, og,
    sg, dq, dk,
    w, qv, kv, xv, ogv, qnext, kt, vals, xh, xmirror, weight, prob, grx, out, skip, acc, vgi, vg,
    stat, statrx, factor, bias, dprob, delta, deltarx, dqown, dqnext, dqrx, pass1, pass2, pass3, pass4,
    lsem, wsem, qsend, qrecv, e1send, e1recv, e2send, e2recv, e3send, e3recv, tsend, trecv, msend, mrecv, zsend, zrecv, rsend, rrecv, isend,
    gsend, grecv, ssend, srecv, esend, erecv, dsend, drecv, f1send, f1recv, f2send, f2recv, f3send, f3recv, go_z, go_r,
):
    s = lax.axis_index("section")
    i = lax.axis_index("seq")
    cy = lax.div(i, SIDE * SIDE)
    cz = lax.rem(lax.div(i, SIDE), SIDE)
    cx = lax.rem(i, SIDE)
    after = lax.rem(i + 1, blocks)
    before = lax.rem(i + blocks - 1, blocks)
    top = sections - 1
    half = sections // 2
    mirror_s = top - s
    step = width // CHUNKS
    per = step // HEAD
    scale = 1.0 / math.sqrt(HEAD)

    def at(y, z, x_):
        return y * (SIDE * SIDE) + z * SIDE + x_

    def copy(src, dst, send, recv, device):
        return pltpu.make_async_remote_copy(
            src_ref=src, dst_ref=dst, send_sem=send, recv_sem=recv,
            device_id=device, device_id_type=MESH,
        )


    def local_copy(n):
        src, dst = ((q.at[0], qv), (k.at[0], kv), (x.at[0], xv), (og, ogv))[n]
        return pltpu.make_async_copy(src, dst, lsem.at[n])


    def shard_copy(a, b):
        src = (wo if a == 0 else wv).at[0, :, pl.ds(b * HEAD, HEAD)]
        return pltpu.make_async_copy(src, w.at[a, cy, cz, cx, b], wsem.at[a, b])

    def columns_of(part, first, count, rows):
        blocks_of = [part(first + n).reshape(rows, HEAD) for n in range(count)]
        return jnp.concatenate(blocks_of, 1)

    def query_copy(m):
        return copy(q.at[0, m], qnext.at[m], qsend.at[m], qrecv.at[m], (s, before))


    quarter = ROWS // SIDE
    back = lax.rem(i + blocks - SIDE, blocks)

    def edge_out(j):
        src = q.at[0, :, pl.ds(j * quarter, quarter)]
        return copy(src, pass1, e1send.at[j], e1recv.at[0], (s, i + j))

    def edge_over(first, last):
        src = q.at[0, :, pl.ds(0, quarter)] if first else pass1
        if last:
            dst, sem = qnext.at[:, pl.ds((SIDE - 1) * quarter, quarter)], e3recv.at[SIDE - 1]
        else:
            dst, sem = pass2, e2recv.at[0]
        return copy(src, dst, e2send.at[0], sem, (s, back))

    def edge_in():
        rows = pl.ds(pl.multiple_of(cx * quarter, quarter), quarter)
        to = i - cx + SIDE - 1
        return copy(pass2, qnext.at[:, rows], e3send.at[0], e3recv.at[cx], (s, to))

    def edge_arrival(j):
        part = qnext.at[:, pl.ds(j * quarter, quarter)]
        return copy(part, part, e3send.at[0], e3recv.at[j], (s, i))

    def stat_copy(m, side):
        to = before if side == 0 else after
        return copy(
            stat.at[m, side], statrx.at[m, 1 - side], tsend.at[m, side], trecv.at[m, 1 - side], (s, to)
        )

    def delta_copy(m, side):
        to = before if side == 0 else after
        return copy(
            delta.at[m, side], deltarx.at[m, 1 - side], esend.at[m, side], erecv.at[m, 1 - side], (s, to)
        )

    def mirror_copy():
        return copy(x.at[0], xmirror, msend.at[0], mrecv.at[0], (mirror_s, i))

    def z_copy(a, d):
        to = at(cy, lax.rem(cz + d, SIDE), cx)
        piece = w.at[a, cy, cz, cx]
        return copy(piece, piece, zsend.at[a, d - 1], zrecv.at[a, d - 1], (s, to))

    def z_arrival(a, d):
        piece = w.at[a, cy, lax.rem(cz + SIDE - d, SIDE), cx]
        return copy(piece, piece, zsend.at[a, d - 1], zrecv.at[a, d - 1], (s, i))

    def slab(a, h, phase, c, part):
        zs = pl.ds(2 * h, 2) if part is None else 2 * h + part
        if phase == 0:
            return w.at[a, cy, zs, c] if h == 0 else w.at[a, c, zs, cx]
        return w.at[a, c, zs] if h == 0 else w.at[a, :, zs, c]

    def kinds(h, phase):
        return (2,) if phase == h else (2, 3)

    def ring(a, h, phase, kind, arrival=False):
        along_x = phase == h
        me = cx if along_x else cy
        plus, minus = lax.rem(me + 1, SIDE), lax.rem(me + SIDE - 1, SIDE)
        across = lax.rem(me + 2, SIDE)
        part = None if kind < 2 or along_x else kind - 2
        if arrival:
            held = (minus, plus, across, across)[kind]
        else:
            held = (me, me, minus, plus)[kind]
        goes = plus if kind % 2 == 0 else minus
        to = at(cy, cz, goes) if along_x else at(goes, cz, cx)
        piece = slab(a, h, phase, held, part)
        sems = (a, h, phase, kind)
        return copy(piece, piece, rsend.at[sems], rrecv.at[sems], (s, to))

    def init_copy(m, c):
        return copy(
            grx.at[m, 0, c], grx.at[m, 1, c], isend.at[m, c], grecv.at[m, 1, c], (s, before)
        )

    def grad_copy(m, c, j):
        to = (s - 1, i) if j == 0 else (s - 1, before)
        return copy(out.at[m, c], grx.at[m, j, c], gsend.at[m, j, c], grecv.at[m, j, c], to)

    def skip_copy(m):
        return copy(out.at[m], skip.at[m], ssend.at[m], srecv.at[m], (mirror_s, i))

    def dq_copy(m):
        return copy(dqnext.at[m], dqrx.at[m], dsend.at[m], drecv.at[m], (s, after))


    ahead = lax.rem(i + SIDE, blocks)

    def dq_part(ref, m, j):
        return ref.at[m, pl.ds(j * step, step)]

    def dq_out(m, j):
        to = i - SIDE + 1 + j
        return copy(dq_part(dqnext, m, j), pass3.at[m], f1send.at[m, j], f1recv.at[m], (s, to))

    def dq_over(m, first, last):
        src = dq_part(dqnext, m, SIDE - 1) if first else pass3.at[m]
        if last:
            return copy(src, dq_part(dqrx, m, 0), f2send.at[m], f3recv.at[m, 0], (s, ahead))
        return copy(src, pass4.at[m], f2send.at[m], f2recv.at[m], (s, ahead))

    def dq_in(m):
        rows = pl.ds(pl.multiple_of(cx * step, step), step)
        return copy(pass4.at[m], dqrx.at[m, rows], f3send.at[m], f3recv.at[m, cx], (s, i - cx))

    def dq_arrival(m, j):
        part = dq_part(dqrx, m, j)
        return copy(part, part, f3send.at[m], f3recv.at[m, j], (s, i))

    for a in range(2):
        for b in range(width // HEAD):
            shard_copy(a, b).start()
    for n in range(3):
        local_copy(n).start()

    @pl.when(s == top)
    def _():
        local_copy(3).start()


    barrier = pltpu.get_barrier_semaphore()

    def greet(section, seq):
        pl.semaphore_signal(barrier, inc=1, device_id=(section, seq), device_id_type=MESH)

    greet(s, after)
    greet(s, before)
    greet(mirror_s, i)
    for d in range(1, SIDE):
        greet(s, at(cy, lax.rem(cz + d, SIDE), cx))
        greet(s, at(cy, cz, lax.rem(cx + d, SIDE)))
    for d in (1, SIDE - 1):
        greet(s, at(lax.rem(cy + d, SIDE), cz, cx))
        greet(s, lax.rem(i + d * SIDE + (blocks - SIDE * SIDE if d > 1 else 0), blocks))

    @pl.when(s > 0)
    def _():
        greet(s - 1, i)
        greet(s - 1, before)

    @pl.when(s < top)
    def _():
        greet(s + 1, i)
        greet(s + 1, after)

    @pl.when(s > 1)
    def _():
        greet(s - 2, i)

    @pl.when(s < top - 1)
    def _():
        greet(s + 2, i)

    odd = lax.rem(s, 2) == 1
    peers = 13 + lax.div(s + 6, sections) + lax.div(2 * top - 1 - s, sections) + 2 * lax.div(s + top, sections) + 2 * lax.div(2 * top - s, sections)
    pl.semaphore_wait(barrier, peers)


    row = lax.broadcasted_iota(jnp.int32, (ROWS, 2 * ROWS), 0)
    col = lax.broadcasted_iota(jnp.int32, (ROWS, 2 * ROWS), 1)
    no_next = jnp.where(i == blocks - 1, 2 * ROWS, 0)
    allowed = ((col < ROWS) & (row <= col)) | ((col >= ROWS) & (row > col - ROWS + no_next))
    bias[...] = jnp.where(allowed, 0.0, -1e30)

    def each_head(body):
        for h in range(HEADS):
            body(h, slice(h * HEAD, (h + 1) * HEAD))

    def soft_in(m):
        @pl.when(cx < SIDE - 1)
        def _():
            query_copy(m).wait_recv()

        def head(h, cols):
            keys = kv[m, :, cols]
            queries = jnp.concatenate([qv[m, :, cols], qnext[m, :, cols]], 0)
            score = dot(keys, queries, NT) * scale + bias[...]
            high = jnp.maximum(jnp.max(score, axis=0, keepdims=True), -1e29)
            e = jnp.exp(score - high)
            total = jnp.sum(e, axis=0, keepdims=True)
            weight[m, h] = e
            one = slice(h, h + 1)
            stat[m, 0, 0, one] = high[:, :ROWS]
            stat[m, 1, 0, one] = high[:, ROWS:]
            stat[m, 0, 1, one] = total[:, :ROWS]
            stat[m, 1, 1, one] = total[:, ROWS:]
            kt[m, cols] = keys.T

        each_head(head)
        for side in range(2):
            stat_copy(m, side).start()

    def soft_out(m):
        for side in range(2):
            stat_copy(m, 1 - side).wait_recv()
            here, there = stat[m, side, 0], statrx[m, side, 0]
            high = jnp.maximum(here, there)
            mine = jnp.exp(here - high)
            total = stat[m, side, 1] * mine + statrx[m, side, 1] * jnp.exp(there - high)
            factor[side] = mine / total

        def head(h, cols):
            one = slice(h, h + 1)
            part = jnp.concatenate([factor[0, one], factor[1, one]], 1)
            p = (weight[m, h] * part).astype(BF16)
            prob[m, h, 0] = p[:, :ROWS]
            prob[m, h, 1] = p[:, ROWS:]

        each_head(head)

    def values():
        @pl.when(s >= half)
        def _():
            mirror_copy().wait_recv()
            xh[...] = (xv[...].astype(F32) + xmirror[...].astype(F32)).astype(BF16)

        @pl.when(s < half)
        def _():
            xh[...] = xv[...]

        def columns(c, carry):
            part = columns_of(lambda b: w[1, :, :, :, b], c * per, per, width)
            result = dot(xh[...].reshape(2 * ROWS, width), part).astype(BF16)
            for m in range(2):
                for u in range(per):
                    block = result[m * ROWS:(m + 1) * ROWS, u * HEAD:(u + 1) * HEAD]
                    vals[m, c * per + u] = block
            return carry

        lax.fori_loop(0, CHUNKS, columns, 0)

    def chain_in(m):
        acc[...] = jnp.zeros_like(acc)

        @pl.when((s < top) & (lax.rem(s, 2) == 0))
        def _():
            for c in range(CHUNKS):
                grad_copy(m, c, 0).wait_recv()

        @pl.when((s < top) & (lax.rem(s, 2) == 1))
        def _():
            for c in range(CHUNKS):
                grad_copy(m, c, 0).wait_recv()
                init_copy(m, c).start()

        def chunk(c, carry):
            grad_copy(m, c, 1).wait_recv()
            both = jnp.concatenate([grx[m, 0, c], grx[m, 1, c]], 1)
            part = columns_of(lambda b: w[0, :, :, :, b], c * per, per, width)
            acc[...] += dot(part, both)
            return carry

        lax.fori_loop(0, CHUNKS, chunk, 0)
        vgi[m, 0] = acc[:, :ROWS].astype(BF16)
        vgi[m, 1] = acc[:, ROWS:].astype(BF16)

    def chain_out(m):
        for h in range(HEADS):
            rows = slice(h * HEAD, (h + 1) * HEAD)
            grad = jnp.concatenate([vgi[m, 0, rows], vgi[m, 1, rows]], 1)
            p = jnp.concatenate([prob[m, h, 0], prob[m, h, 1]], 1)
            vg[rows] = dot(grad, p, NT).astype(BF16)

        @pl.when(s < half - 1)
        def _():
            skip_copy(m).wait_recv()

        @pl.when(s == half - 1)
        def _():
            skip[m] = grx[m, 0]

        def chunk(c, carry):
            part = columns_of(lambda b: w[1, c, :, :, b], 0, width // HEAD, step)
            total = dot(part, vg[...]) + grx[m, 0, c].astype(F32) + skip[m, c].astype(F32)
            out[m, c] = total.astype(BF16)

            @pl.when(lax.rem(s, 2) == 1)
            def _():
                grad_copy(m, c, 1).start()

            @pl.when(s > 0)
            def _():
                grad_copy(m, c, 0).start()

            return carry

        lax.fori_loop(0, CHUNKS, chunk, 0)

        @pl.when(s > half)
        def _():
            skip_copy(m).start()

    def post_in(m):
        def head(h, cols):
            both = jnp.concatenate([vgi[m, 0, cols], vgi[m, 1, cols]], 1)
            grad = dot(vals[m, h], both)
            dprob[m, h] = grad
            p = jnp.concatenate([prob[m, h, 0], prob[m, h, 1]], 1).astype(F32)
            total = jnp.sum(p * grad, axis=0, keepdims=True)
            one = slice(h, h + 1)
            delta[m, 0, one] = total[:, :ROWS]
            delta[m, 1, one] = total[:, ROWS:]

        each_head(head)
        for side in range(2):
            delta_copy(m, side).start()

    def post_out(m):
        for side in range(2):
            delta_copy(m, 1 - side).wait_recv()
            factor[side] = delta[m, side] + deltarx[m, side]

        def head(h, cols):
            one = slice(h, h + 1)
            whole = jnp.concatenate([factor[0, one], factor[1, one]], 1)
            p = jnp.concatenate([prob[m, h, 0], prob[m, h, 1]], 1).astype(F32)
            ds = (p * (dprob[m, h] - whole) * scale).astype(BF16)
            queries = jnp.concatenate([qv[m, :, cols], qnext[m, :, cols]], 0)
            dk[0, m, :, cols] = dot(ds, queries).astype(BF16)
            both = dot(kt[m, cols], ds)
            dqown[m, cols] = both[:, :ROWS]
            dqnext[m, cols] = both[:, ROWS:].astype(BF16)

        each_head(head)

        @pl.when(cx < SIDE - 1)
        def _():
            dq_copy(m).start()

        @pl.when(cx == SIDE - 1)
        def _():
            for j in range(SIDE - 1):
                dq_out(m, j).start()
            dq_over(m, True, False).start()


    def relay(a, phase):
        for h in range(2):
            for kind in range(2):
                ring(a, h, phase, kind, True).wait_recv()
                if kind + 2 in kinds(h, phase):
                    ring(a, h, phase, kind + 2).start()

    def settle(a, phase):
        for h in range(2):
            for kind in kinds(h, phase):
                ring(a, h, phase, kind, True).wait_recv()

    def second():
        for a in range(2):
            settle(a, 0)
            for h in range(2):
                for kind in range(2):
                    ring(a, h, 1, kind).start()

    def each_micro(body):
        def turn(m, carry):
            body(m)
            return carry

        lax.fori_loop(0, 2, turn, 0)

    def start_queries():
        @pl.when(cx == 0)
        def _():
            for j in range(1, SIDE):
                edge_out(j).start()
            edge_over(True, False).start()

        @pl.when(cx > 0)
        def _():
            for m in range(2):
                query_copy(m).start()

    def edge_first():
        @pl.when(cx > 0)
        def _():
            edge_out(0).wait_recv()

        @pl.when((cx > 0) & (cx < SIDE - 1))
        def _():
            edge_over(False, False).start()

        @pl.when(cx == SIDE - 1)
        def _():
            edge_over(False, True).start()

    def edge_second():
        @pl.when(cx < SIDE - 1)
        def _():
            edge_over(False, False).wait_recv()
            edge_in().start()

    @pl.when(s < top - 1)
    def _():
        pl.semaphore_wait(go_z, 1)

    for a in range(2):
        for b in range(width // HEAD):
            shard_copy(a, b).wait()
        for d in range(1, SIDE):
            z_copy(a, d).start()

    start_queries()

    for n in range(3):
        local_copy(n).wait()

    for a in range(2):
        for d in range(1, SIDE):
            z_arrival(a, d).wait_recv()
        for h in range(2):
            for kind in range(2):
                ring(a, h, 0, kind).start()

    @pl.when(s > 1)
    def _():
        pl.semaphore_signal(go_z, inc=1, device_id=(s - 2, i), device_id_type=MESH)

    edge_first()

    for a in range(2):
        relay(a, 0)

    edge_second()

    @pl.when(odd)
    def _():
        second()
        for a in range(2):
            relay(a, 1)
        pl.semaphore_signal(go_r, inc=1, device_id=(s - 1, i), device_id_type=MESH)

    @pl.when(s == top)
    def _():
        local_copy(3).wait()
        for m in range(2):
            for c in range(CHUNKS):
                grx[m, 0, c] = ogv[m, :, c * step:(c + 1) * step].T
                init_copy(m, c).start()

    @pl.when(s >= half)
    def _():
        skip[...] = jnp.zeros_like(skip)

    @pl.when(cx == SIDE - 1)
    def _():
        for j in range(SIDE):
            edge_arrival(j).wait_recv()

    each_micro(soft_in)

    each_micro(soft_out)

    @pl.when(jnp.logical_not(odd))
    def _():
        pl.semaphore_wait(go_r, 1)
        second()
        for a in range(2):
            relay(a, 1)

    settle(0, 1)
    settle(1, 1)

    @pl.when(s < half)
    def _():
        mirror_copy().start()

    def turn(t, carry):
        m = lax.rem(t, 2)
        early = (t < 2) & (s == 0)

        @pl.when(((t == 0) & (s < half)) | ((t == 2) & (s >= half)))
        def _():
            values()

        @pl.when(t < 2)
        def _():
            chain_in(m)

        @pl.when(early | ((t >= 2) & (t < 4) & (s > 0)))
        def _():
            post_in(m)

        @pl.when(t < 2)
        def _():
            chain_out(m)

        @pl.when(early | ((t >= 4) & (s > 0)))
        def _():
            post_out(m)

        return carry

    lax.fori_loop(0, 6, turn, 0)

    for m in range(2):
        @pl.when(cx < SIDE - 1)
        def _():
            dq_out(m, 0).wait_recv()

        @pl.when((cx > 0) & (cx < SIDE - 1))
        def _():
            dq_over(m, False, False).start()

        @pl.when(cx == 0)
        def _():
            dq_over(m, False, True).start()

    for m in range(2):
        @pl.when(cx > 0)
        def _():
            dq_over(m, False, False).wait_recv()
            dq_in(m).start()

    for m in range(2):
        for c in range(CHUNKS):
            sg[0, m, :, c * step:(c + 1) * step] = out[m, c].T
    for m in range(2):
        @pl.when(cx > 0)
        def _():
            dq_copy(m).wait_recv()

        @pl.when(cx == 0)
        def _():
            for j in range(SIDE):
                dq_arrival(m, j).wait_recv()

        for c in range(CHUNKS):
            rows = slice(c * step, (c + 1) * step)
            dq[0, m, :, rows] = (dqown[m, rows] + dqrx[m, rows].astype(F32)).astype(BF16).T


    @pl.when(cx == 0)
    def _():
        for j in range(1, SIDE):
            edge_out(j).wait_send()

    @pl.when(cx > 0)
    def _():
        for m in range(2):
            query_copy(m).wait_send()

    edge_over(False, False).wait_send()

    @pl.when(cx < SIDE - 1)
    def _():
        edge_in().wait_send()

    for m in range(2):
        @pl.when(cx < SIDE - 1)
        def _():
            dq_copy(m).wait_send()

        @pl.when(cx == SIDE - 1)
        def _():
            for j in range(SIDE - 1):
                dq_out(m, j).wait_send()

        dq_over(m, False, False).wait_send()

        @pl.when(cx > 0)
        def _():
            dq_in(m).wait_send()

        for side in range(2):
            stat_copy(m, side).wait_send()
            delta_copy(m, side).wait_send()
    for a in range(2):
        for d in range(1, SIDE):
            z_copy(a, d).wait_send()
        for h in range(2):
            for phase in range(2):
                for kind in (0, 1) + kinds(h, phase):
                    ring(a, h, phase, kind).wait_send()

    @pl.when(s < half)
    def _():
        mirror_copy().wait_send()

    @pl.when(odd)
    def _():
        for m in range(2):
            for c in range(CHUNKS):
                init_copy(m, c).wait_send()
                grad_copy(m, c, 1).wait_send()

    @pl.when(s > 0)
    def _():
        for m in range(2):
            for c in range(CHUNKS):
                grad_copy(m, c, 0).wait_send()

    @pl.when(s > half)
    def _():
        for m in range(2):
            skip_copy(m).wait_send()


def per_device(x_saved, queries, keys, value_weight, out_weight, out_grad):
    sections = lax.axis_size("section")
    blocks = lax.axis_size("seq")
    micro, rows, width = out_grad.shape
    shape = jax.ShapeDtypeStruct((1, micro, rows, width), BF16)
    step = width // CHUNKS
    vmem = pl.BlockSpec(memory_space=pltpu.VMEM)
    hbm = pl.BlockSpec(memory_space=pltpu.HBM)
    dma = pltpu.SemaphoreType.DMA
    block = pltpu.VMEM((micro, rows, width), BF16)
    turned = pltpu.VMEM((micro, width, rows), BF16)
    chunks = pltpu.VMEM((micro, CHUNKS, step, rows), BF16)
    side_rows = pltpu.VMEM((micro, 2, HEADS, rows), F32)
    return pl.pallas_call(
        functools.partial(kernel, sections, blocks, width),
        out_shape=(shape, shape, shape),
        in_specs=[hbm] * 6,
        out_specs=(vmem,) * 3,
        scratch_shapes=[
            pltpu.VMEM((2, SIDE, SIDE, SIDE, width // HEAD, width // blocks, HEAD), BF16),
            block,
            block,
            block,
            block,
            block,
            turned,
            pltpu.VMEM((micro, HEADS, rows, HEAD), BF16),
            block,
            block,
            pltpu.VMEM((micro, HEADS, rows, 2 * rows), F32),
            pltpu.VMEM((micro, HEADS, 2, rows, rows), BF16),
            pltpu.VMEM((micro, 2, CHUNKS, step, rows), BF16),
            chunks,
            chunks,
            pltpu.VMEM((width, 2 * rows), F32),
            pltpu.VMEM((micro, 2, width, rows), BF16),
            pltpu.VMEM((width, rows), BF16),
            pltpu.VMEM((micro, 2, 2, HEADS, rows), F32),
            pltpu.VMEM((micro, 2, 2, HEADS, rows), F32),
            pltpu.VMEM((2, HEADS, rows), F32),
            pltpu.VMEM((rows, 2 * rows), F32),
            pltpu.VMEM((micro, HEADS, rows, 2 * rows), F32),
            side_rows,
            side_rows,
            pltpu.VMEM((micro, width, rows), F32),
            turned,
            turned,
            pltpu.VMEM((micro, rows // SIDE, width), BF16),
            pltpu.VMEM((micro, rows // SIDE, width), BF16),
            pltpu.VMEM((micro, step, rows), BF16),
            pltpu.VMEM((micro, step, rows), BF16),
            dma((4,)), dma((2, width // HEAD)),
            dma((2,)), dma((2,)),
            dma((SIDE,)), dma((1,)),
            dma((1,)), dma((1,)),
            dma((1,)), dma((SIDE,)),
            dma((2, 2)), dma((2, 2)),
            dma((1,)), dma((1,)),
            dma((2, 3)), dma((2, 3)),
            dma((2, 2, 2, 4)), dma((2, 2, 2, 4)),
            dma((2, CHUNKS)),
            dma((2, 2, CHUNKS)), dma((2, 2, CHUNKS)),
            dma((2,)), dma((2,)),
            dma((2, 2)), dma((2, 2)),
            dma((2,)), dma((2,)),
            dma((2, SIDE)), dma((2,)),
            dma((2,)), dma((2,)),
            dma((2,)), dma((2, SIDE)),
            pltpu.SemaphoreType.REGULAR,
            pltpu.SemaphoreType.REGULAR,
        ],
        compiler_params=pltpu.CompilerParams(
            collective_id=0, has_side_effects=True, vmem_limit_bytes=60 * 2**20
        ),
        cost_estimate=pl.CostEstimate(flops=4 * 10**9, bytes_accessed=8 * 2**20, transcendentals=2**19),
        name="backward",
    )(x_saved, queries, keys, value_weight, out_weight, out_grad)


def solution(mesh):
    rows = P("section", None, "seq", None)
    weights = P("section", "seq", None)
    return jax.shard_map(
        per_device,
        mesh=mesh,
        in_specs=(rows, rows, rows, weights, weights, P(None, "seq", None)),
        out_specs=(rows, rows, rows),
        check_vma=False,
    )
```

```python
import functools
import math

import jax
import jax.numpy as jnp
from jax import lax
from jax.experimental import pallas as pl
from jax.experimental.pallas import tpu as pltpu
from jax.sharding import PartitionSpec as P

MESH = pl.DeviceIdType.MESH
HEADS = 8
HEAD = 128
ROWS = 128
SIDE = 4
CHUNKS = 4
BF16 = jnp.bfloat16
F32 = jnp.float32
NN = (((1,), (0,)), ((), ()))
NT = (((1,), (1,)), ((), ()))


def dot(left, right, dims=NN):
    return lax.dot_general(left, right, dims, preferred_element_type=F32)


def kernel(
    sections, blocks, width,
    x, q, k, wv, wo, og,
    sg, dq, dk,
    w, qv, kv, xv, ogv, qnext, kt, vals, xh, xmirror, weight, prob, grx, out, skip, acc, vgi, vg,
    stat, statrx, factor, bias, dprob, delta, deltarx, dqown, dqnext, dqrx, pass1, pass2, pass3, pass4,
    lsem, wsem, qsend, qrecv, e1send, e1recv, e2send, e2recv, e3send, e3recv, tsend, trecv, msend, mrecv, zsend, zrecv, rsend, rrecv, isend,
    gsend, grecv, ssend, srecv, esend, erecv, dsend, drecv, f1send, f1recv, f2send, f2recv, f3send, f3recv, go_z, go_r,
):
    s = lax.axis_index("section")
    i = lax.axis_index("seq")
    cy = lax.div(i, SIDE * SIDE)
    cz = lax.rem(lax.div(i, SIDE), SIDE)
    cx = lax.rem(i, SIDE)
    after = lax.rem(i + 1, blocks)
    before = lax.rem(i + blocks - 1, blocks)
    top = sections - 1
    half = sections // 2
    mirror_s = top - s
    step = width // CHUNKS
    per = step // HEAD
    scale = 1.0 / math.sqrt(HEAD)

    def at(y, z, x_):
        return y * (SIDE * SIDE) + z * SIDE + x_

    def copy(src, dst, send, recv, device):
        return pltpu.make_async_remote_copy(
            src_ref=src, dst_ref=dst, send_sem=send, recv_sem=recv,
            device_id=device, device_id_type=MESH,
        )


    def local_copy(n):
        src, dst = ((q.at[0], qv), (k.at[0], kv), (x.at[0], xv), (og, ogv))[n]
        return pltpu.make_async_copy(src, dst, lsem.at[n])


    def shard_copy(a, b):
        src = (wo if a == 0 else wv).at[0, :, pl.ds(b * HEAD, HEAD)]
        return pltpu.make_async_copy(src, w.at[a, cy, cz, cx, b], wsem.at[a, b])

    def columns_of(part, first, count, rows):
        blocks_of = [part(first + n).reshape(rows, HEAD) for n in range(count)]
        return jnp.concatenate(blocks_of, 1)

    def query_copy(m):
        return copy(q.at[0, m], qnext.at[m], qsend.at[m], qrecv.at[m], (s, before))


    quarter = ROWS // SIDE
    back = lax.rem(i + blocks - SIDE, blocks)

    def edge_out(j):
        src = q.at[0, :, pl.ds(j * quarter, quarter)]
        return copy(src, pass1, e1send.at[j], e1recv.at[0], (s, i + j))

    def edge_over(first, last):
        src = q.at[0, :, pl.ds(0, quarter)] if first else pass1
        if last:
            dst, sem = qnext.at[:, pl.ds((SIDE - 1) * quarter, quarter)], e3recv.at[SIDE - 1]
        else:
            dst, sem = pass2, e2recv.at[0]
        return copy(src, dst, e2send.at[0], sem, (s, back))

    def edge_in():
        rows = pl.ds(pl.multiple_of(cx * quarter, quarter), quarter)
        to = i - cx + SIDE - 1
        return copy(pass2, qnext.at[:, rows], e3send.at[0], e3recv.at[cx], (s, to))

    def edge_arrival(j):
        part = qnext.at[:, pl.ds(j * quarter, quarter)]
        return copy(part, part, e3send.at[0], e3recv.at[j], (s, i))

    def stat_copy(m, side):
        to = before if side == 0 else after
        return copy(
            stat.at[m, side], statrx.at[m, 1 - side], tsend.at[m, side], trecv.at[m, 1 - side], (s, to)
        )

    def delta_copy(m, side):
        to = before if side == 0 else after
        return copy(
            delta.at[m, side], deltarx.at[m, 1 - side], esend.at[m, side], erecv.at[m, 1 - side], (s, to)
        )

    def mirror_copy():
        return copy(x.at[0], xmirror, msend.at[0], mrecv.at[0], (mirror_s, i))

    def z_copy(a, d):
        to = at(cy, lax.rem(cz + d, SIDE), cx)
        piece = w.at[a, cy, cz, cx]
        return copy(piece, piece, zsend.at[a, d - 1], zrecv.at[a, d - 1], (s, to))

    def z_arrival(a, d):
        piece = w.at[a, cy, lax.rem(cz + SIDE - d, SIDE), cx]
        return copy(piece, piece, zsend.at[a, d - 1], zrecv.at[a, d - 1], (s, i))

    def slab(a, h, phase, c, part):
        zs = pl.ds(2 * h, 2) if part is None else 2 * h + part
        if phase == 0:
            return w.at[a, cy, zs, c] if h == 0 else w.at[a, c, zs, cx]
        return w.at[a, c, zs] if h == 0 else w.at[a, :, zs, c]

    def kinds(h, phase):
        return (2,) if phase == h else (2, 3)

    def ring(a, h, phase, kind, arrival=False):
        along_x = phase == h
        me = cx if along_x else cy
        plus, minus = lax.rem(me + 1, SIDE), lax.rem(me + SIDE - 1, SIDE)
        across = lax.rem(me + 2, SIDE)
        part = None if kind < 2 or along_x else kind - 2
        if arrival:
            held = (minus, plus, across, across)[kind]
        else:
            held = (me, me, minus, plus)[kind]
        goes = plus if kind % 2 == 0 else minus
        to = at(cy, cz, goes) if along_x else at(goes, cz, cx)
        piece = slab(a, h, phase, held, part)
        sems = (a, h, phase, kind)
        return copy(piece, piece, rsend.at[sems], rrecv.at[sems], (s, to))

    def init_copy(m, c):
        return copy(
            grx.at[m, 0, c], grx.at[m, 1, c], isend.at[m, c], grecv.at[m, 1, c], (s, before)
        )

    def grad_copy(m, c, j):
        to = (s - 1, i) if j == 0 else (s - 1, before)
        return copy(out.at[m, c], grx.at[m, j, c], gsend.at[m, j, c], grecv.at[m, j, c], to)

    def skip_copy(m):
        return copy(out.at[m], skip.at[m], ssend.at[m], srecv.at[m], (mirror_s, i))

    def dq_copy(m):
        return copy(dqnext.at[m], dqrx.at[m], dsend.at[m], drecv.at[m], (s, after))


    ahead = lax.rem(i + SIDE, blocks)

    def dq_part(ref, m, j):
        return ref.at[m, pl.ds(j * step, step)]

    def dq_out(m, j):
        to = i - SIDE + 1 + j
        return copy(dq_part(dqnext, m, j), pass3.at[m], f1send.at[m, j], f1recv.at[m], (s, to))

    def dq_over(m, first, last):
        src = dq_part(dqnext, m, SIDE - 1) if first else pass3.at[m]
        if last:
            return copy(src, dq_part(dqrx, m, 0), f2send.at[m], f3recv.at[m, 0], (s, ahead))
        return copy(src, pass4.at[m], f2send.at[m], f2recv.at[m], (s, ahead))

    def dq_in(m):
        rows = pl.ds(pl.multiple_of(cx * step, step), step)
        return copy(pass4.at[m], dqrx.at[m, rows], f3send.at[m], f3recv.at[m, cx], (s, i - cx))

    def dq_arrival(m, j):
        part = dq_part(dqrx, m, j)
        return copy(part, part, f3send.at[m], f3recv.at[m, j], (s, i))

    for a in range(2):
        for b in range(width // HEAD):
            shard_copy(a, b).start()
    for n in range(3):
        local_copy(n).start()

    @pl.when(s == top)
    def _():
        local_copy(3).start()


    barrier = pltpu.get_barrier_semaphore()

    def greet(section, seq):
        pl.semaphore_signal(barrier, inc=1, device_id=(section, seq), device_id_type=MESH)

    greet(s, after)
    greet(s, before)
    greet(mirror_s, i)
    for d in range(1, SIDE):
        greet(s, at(cy, lax.rem(cz + d, SIDE), cx))
        greet(s, at(cy, cz, lax.rem(cx + d, SIDE)))
    for d in (1, SIDE - 1):
        greet(s, at(lax.rem(cy + d, SIDE), cz, cx))
        greet(s, lax.rem(i + d * SIDE + (blocks - SIDE * SIDE if d > 1 else 0), blocks))

    @pl.when(s > 0)
    def _():
        greet(s - 1, i)
        greet(s - 1, before)

    @pl.when(s < top)
    def _():
        greet(s + 1, i)
        greet(s + 1, after)

    @pl.when(s > 1)
    def _():
        greet(s - 2, i)

    @pl.when(s < top - 1)
    def _():
        greet(s + 2, i)

    odd = lax.rem(s, 2) == 1
    peers = 13 + lax.div(s + 6, sections) + lax.div(2 * top - 1 - s, sections) + 2 * lax.div(s + top, sections) + 2 * lax.div(2 * top - s, sections)
    pl.semaphore_wait(barrier, peers)


    row = lax.broadcasted_iota(jnp.int32, (ROWS, 2 * ROWS), 0)
    col = lax.broadcasted_iota(jnp.int32, (ROWS, 2 * ROWS), 1)
    no_next = jnp.where(i == blocks - 1, 2 * ROWS, 0)
    allowed = ((col < ROWS) & (row <= col)) | ((col >= ROWS) & (row > col - ROWS + no_next))
    bias[...] = jnp.where(allowed, 0.0, -1e30)

    def each_head(body):
        for h in range(HEADS):
            body(h, slice(h * HEAD, (h + 1) * HEAD))

    def soft_in(m):
        @pl.when(cx < SIDE - 1)
        def _():
            query_copy(m).wait_recv()

        def head(h, cols):
            keys = kv[m, :, cols]
            queries = jnp.concatenate([qv[m, :, cols], qnext[m, :, cols]], 0)
            score = dot(keys, queries, NT) * scale + bias[...]
            high = jnp.maximum(jnp.max(score, axis=0, keepdims=True), -1e29)
            e = jnp.exp(score - high)
            total = jnp.sum(e, axis=0, keepdims=True)
            weight[m, h] = e
            one = slice(h, h + 1)
            stat[m, 0, 0, one] = high[:, :ROWS]
            stat[m, 1, 0, one] = high[:, ROWS:]
            stat[m, 0, 1, one] = total[:, :ROWS]
            stat[m, 1, 1, one] = total[:, ROWS:]
            kt[m, cols] = keys.T

        each_head(head)
        for side in range(2):
            stat_copy(m, side).start()

    def soft_out(m):
        for side in range(2):
            stat_copy(m, 1 - side).wait_recv()
            here, there = stat[m, side, 0], statrx[m, side, 0]
            high = jnp.maximum(here, there)
            mine = jnp.exp(here - high)
            total = stat[m, side, 1] * mine + statrx[m, side, 1] * jnp.exp(there - high)
            factor[side] = mine / total

        def head(h, cols):
            one = slice(h, h + 1)
            part = jnp.concatenate([factor[0, one], factor[1, one]], 1)
            p = (weight[m, h] * part).astype(BF16)
            prob[m, h, 0] = p[:, :ROWS]
            prob[m, h, 1] = p[:, ROWS:]

        each_head(head)

    def values():
        @pl.when(s >= half)
        def _():
            mirror_copy().wait_recv()
            xh[...] = (xv[...].astype(F32) + xmirror[...].astype(F32)).astype(BF16)

        @pl.when(s < half)
        def _():
            xh[...] = xv[...]

        def columns(c, carry):
            part = columns_of(lambda b: w[1, :, :, :, b], c * per, per, width)
            result = dot(xh[...].reshape(2 * ROWS, width), part).astype(BF16)
            for m in range(2):
                for u in range(per):
                    block = result[m * ROWS:(m + 1) * ROWS, u * HEAD:(u + 1) * HEAD]
                    vals[m, c * per + u] = block
            return carry

        lax.fori_loop(0, CHUNKS, columns, 0)

    def chain_in(m):
        acc[...] = jnp.zeros_like(acc)

        @pl.when((s < top) & (lax.rem(s, 2) == 0))
        def _():
            for c in range(CHUNKS):
                grad_copy(m, c, 0).wait_recv()

        @pl.when((s < top) & (lax.rem(s, 2) == 1))
        def _():
            for c in range(CHUNKS):
                grad_copy(m, c, 0).wait_recv()
                init_copy(m, c).start()

        def chunk(c, carry):
            grad_copy(m, c, 1).wait_recv()
            both = jnp.concatenate([grx[m, 0, c], grx[m, 1, c]], 1)
            part = columns_of(lambda b: w[0, :, :, :, b], c * per, per, width)
            acc[...] += dot(part, both)
            return carry

        lax.fori_loop(0, CHUNKS, chunk, 0)
        vgi[m, 0] = acc[:, :ROWS].astype(BF16)
        vgi[m, 1] = acc[:, ROWS:].astype(BF16)

    def chain_out(m):
        for h in range(HEADS):
            rows = slice(h * HEAD, (h + 1) * HEAD)
            grad = jnp.concatenate([vgi[m, 0, rows], vgi[m, 1, rows]], 1)
            p = jnp.concatenate([prob[m, h, 0], prob[m, h, 1]], 1)
            vg[rows] = dot(grad, p, NT).astype(BF16)

        @pl.when(s < half - 1)
        def _():
            skip_copy(m).wait_recv()

        @pl.when(s == half - 1)
        def _():
            skip[m] = grx[m, 0]

        def chunk(c, carry):
            part = columns_of(lambda b: w[1, c, :, :, b], 0, width // HEAD, step)
            total = dot(part, vg[...]) + grx[m, 0, c].astype(F32) + skip[m, c].astype(F32)
            out[m, c] = total.astype(BF16)

            @pl.when(lax.rem(s, 2) == 1)
            def _():
                grad_copy(m, c, 1).start()

            @pl.when(s > 0)
            def _():
                grad_copy(m, c, 0).start()

            return carry

        lax.fori_loop(0, CHUNKS, chunk, 0)

        @pl.when(s > half)
        def _():
            skip_copy(m).start()

    def post_in(m):
        def head(h, cols):
            both = jnp.concatenate([vgi[m, 0, cols], vgi[m, 1, cols]], 1)
            grad = dot(vals[m, h], both)
            dprob[m, h] = grad
            p = jnp.concatenate([prob[m, h, 0], prob[m, h, 1]], 1).astype(F32)
            total = jnp.sum(p * grad, axis=0, keepdims=True)
            one = slice(h, h + 1)
            delta[m, 0, one] = total[:, :ROWS]
            delta[m, 1, one] = total[:, ROWS:]

        each_head(head)
        for side in range(2):
            delta_copy(m, side).start()

    def post_out(m):
        for side in range(2):
            delta_copy(m, 1 - side).wait_recv()
            factor[side] = delta[m, side] + deltarx[m, side]

        def head(h, cols):
            one = slice(h, h + 1)
            whole = jnp.concatenate([factor[0, one], factor[1, one]], 1)
            p = jnp.concatenate([prob[m, h, 0], prob[m, h, 1]], 1).astype(F32)
            ds = (p * (dprob[m, h] - whole) * scale).astype(BF16)
            queries = jnp.concatenate([qv[m, :, cols], qnext[m, :, cols]], 0)
            dk[0, m, :, cols] = dot(ds, queries).astype(BF16)
            both = dot(kt[m, cols], ds)
            dqown[m, cols] = both[:, :ROWS]
            dqnext[m, cols] = both[:, ROWS:].astype(BF16)

        each_head(head)

        @pl.when(cx < SIDE - 1)
        def _():
            dq_copy(m).start()

        @pl.when(cx == SIDE - 1)
        def _():
            for j in range(SIDE - 1):
                dq_out(m, j).start()
            dq_over(m, True, False).start()


    def relay(a, phase):
        for h in range(2):
            for kind in range(2):
                ring(a, h, phase, kind, True).wait_recv()
                if kind + 2 in kinds(h, phase):
                    ring(a, h, phase, kind + 2).start()

    def settle(a, phase):
        for h in range(2):
            for kind in kinds(h, phase):
                ring(a, h, phase, kind, True).wait_recv()

    def second():
        for a in range(2):
            settle(a, 0)
            for h in range(2):
                for kind in range(2):
                    ring(a, h, 1, kind).start()

    def each_micro(body):
        def turn(m, carry):
            body(m)
            return carry

        lax.fori_loop(0, 2, turn, 0)

    def start_queries():
        @pl.when(cx == 0)
        def _():
            for j in range(1, SIDE):
                edge_out(j).start()
            edge_over(True, False).start()

        @pl.when(cx > 0)
        def _():
            for m in range(2):
                query_copy(m).start()

    def edge_first():
        @pl.when(cx > 0)
        def _():
            edge_out(0).wait_recv()

        @pl.when((cx > 0) & (cx < SIDE - 1))
        def _():
            edge_over(False, False).start()

        @pl.when(cx == SIDE - 1)
        def _():
            edge_over(False, True).start()

    def edge_second():
        @pl.when(cx < SIDE - 1)
        def _():
            edge_over(False, False).wait_recv()
            edge_in().start()

    @pl.when(s < top - 1)
    def _():
        pl.semaphore_wait(go_z, 1)

    for a in range(2):
        for b in range(width // HEAD):
            shard_copy(a, b).wait()
        for d in range(1, SIDE):
            z_copy(a, d).start()

    start_queries()

    for n in range(3):
        local_copy(n).wait()

    for a in range(2):
        for d in range(1, SIDE):
            z_arrival(a, d).wait_recv()
        for h in range(2):
            for kind in range(2):
                ring(a, h, 0, kind).start()

    @pl.when(s > 1)
    def _():
        pl.semaphore_signal(go_z, inc=1, device_id=(s - 2, i), device_id_type=MESH)

    edge_first()

    for a in range(2):
        relay(a, 0)

    edge_second()

    @pl.when(odd)
    def _():
        second()
        for a in range(2):
            relay(a, 1)
        pl.semaphore_signal(go_r, inc=1, device_id=(s - 1, i), device_id_type=MESH)

    @pl.when(s == top)
    def _():
        local_copy(3).wait()
        for m in range(2):
            for c in range(CHUNKS):
                grx[m, 0, c] = ogv[m, :, c * step:(c + 1) * step].T
                init_copy(m, c).start()

    @pl.when(s >= half)
    def _():
        skip[...] = jnp.zeros_like(skip)

    @pl.when(cx == SIDE - 1)
    def _():
        for j in range(SIDE):
            edge_arrival(j).wait_recv()

    each_micro(soft_in)

    each_micro(soft_out)

    @pl.when(jnp.logical_not(odd))
    def _():
        pl.semaphore_wait(go_r, 1)
        second()
        for a in range(2):
            relay(a, 1)

    settle(0, 1)
    settle(1, 1)

    @pl.when(s < half)
    def _():
        mirror_copy().start()

    def turn(t, carry):
        m = lax.rem(t, 2)
        early = (t < 2) & (s == 0)
        late = t - 1 - 3 * lax.div(s + top, sections)

        @pl.when(((t == 0) & (s < half)) | ((t == 2) & (s >= half)))
        def _():
            values()

        @pl.when(t < 2)
        def _():
            chain_in(m)

        @pl.when(early | ((t >= 2) & (t < 4) & (s > 0)))
        def _():
            post_in(m)

        @pl.when(((s == 0) & (t >= 1) & (t <= 2)) | ((s > 0) & (t >= 4)))
        def _():
            post_out(late)

        @pl.when(t < 2)
        def _():
            chain_out(m)

        return carry

    lax.fori_loop(0, 6, turn, 0)

    for m in range(2):
        @pl.when(cx < SIDE - 1)
        def _():
            dq_out(m, 0).wait_recv()

        @pl.when((cx > 0) & (cx < SIDE - 1))
        def _():
            dq_over(m, False, False).start()

        @pl.when(cx == 0)
        def _():
            dq_over(m, False, True).start()

    for m in range(2):
        @pl.when(cx > 0)
        def _():
            dq_over(m, False, False).wait_recv()
            dq_in(m).start()

    for m in range(2):
        for c in range(CHUNKS):
            sg[0, m, :, c * step:(c + 1) * step] = out[m, c].T
    for m in range(2):
        @pl.when(cx > 0)
        def _():
            dq_copy(m).wait_recv()

        @pl.when(cx == 0)
        def _():
            for j in range(SIDE):
                dq_arrival(m, j).wait_recv()

        for c in range(CHUNKS):
            rows = slice(c * step, (c + 1) * step)
            dq[0, m, :, rows] = (dqown[m, rows] + dqrx[m, rows].astype(F32)).astype(BF16).T


    @pl.when(cx == 0)
    def _():
        for j in range(1, SIDE):
            edge_out(j).wait_send()

    @pl.when(cx > 0)
    def _():
        for m in range(2):
            query_copy(m).wait_send()

    edge_over(False, False).wait_send()

    @pl.when(cx < SIDE - 1)
    def _():
        edge_in().wait_send()

    for m in range(2):
        @pl.when(cx < SIDE - 1)
        def _():
            dq_copy(m).wait_send()

        @pl.when(cx == SIDE - 1)
        def _():
            for j in range(SIDE - 1):
                dq_out(m, j).wait_send()

        dq_over(m, False, False).wait_send()

        @pl.when(cx > 0)
        def _():
            dq_in(m).wait_send()

        for side in range(2):
            stat_copy(m, side).wait_send()
            delta_copy(m, side).wait_send()
    for a in range(2):
        for d in range(1, SIDE):
            z_copy(a, d).wait_send()
        for h in range(2):
            for phase in range(2):
                for kind in (0, 1) + kinds(h, phase):
                    ring(a, h, phase, kind).wait_send()

    @pl.when(s < half)
    def _():
        mirror_copy().wait_send()

    @pl.when(odd)
    def _():
        for m in range(2):
            for c in range(CHUNKS):
                init_copy(m, c).wait_send()
                grad_copy(m, c, 1).wait_send()

    @pl.when(s > 0)
    def _():
        for m in range(2):
            for c in range(CHUNKS):
                grad_copy(m, c, 0).wait_send()

    @pl.when(s > half)
    def _():
        for m in range(2):
            skip_copy(m).wait_send()


def per_device(x_saved, queries, keys, value_weight, out_weight, out_grad):
    sections = lax.axis_size("section")
    blocks = lax.axis_size("seq")
    micro, rows, width = out_grad.shape
    shape = jax.ShapeDtypeStruct((1, micro, rows, width), BF16)
    step = width // CHUNKS
    vmem = pl.BlockSpec(memory_space=pltpu.VMEM)
    hbm = pl.BlockSpec(memory_space=pltpu.HBM)
    dma = pltpu.SemaphoreType.DMA
    block = pltpu.VMEM((micro, rows, width), BF16)
    turned = pltpu.VMEM((micro, width, rows), BF16)
    chunks = pltpu.VMEM((micro, CHUNKS, step, rows), BF16)
    side_rows = pltpu.VMEM((micro, 2, HEADS, rows), F32)
    return pl.pallas_call(
        functools.partial(kernel, sections, blocks, width),
        out_shape=(shape, shape, shape),
        in_specs=[hbm] * 6,
        out_specs=(vmem,) * 3,
        scratch_shapes=[
            pltpu.VMEM((2, SIDE, SIDE, SIDE, width // HEAD, width // blocks, HEAD), BF16),
            block,
            block,
            block,
            block,
            block,
            turned,
            pltpu.VMEM((micro, HEADS, rows, HEAD), BF16),
            block,
            block,
            pltpu.VMEM((micro, HEADS, rows, 2 * rows), F32),
            pltpu.VMEM((micro, HEADS, 2, rows, rows), BF16),
            pltpu.VMEM((micro, 2, CHUNKS, step, rows), BF16),
            chunks,
            chunks,
            pltpu.VMEM((width, 2 * rows), F32),
            pltpu.VMEM((micro, 2, width, rows), BF16),
            pltpu.VMEM((width, rows), BF16),
            pltpu.VMEM((micro, 2, 2, HEADS, rows), F32),
            pltpu.VMEM((micro, 2, 2, HEADS, rows), F32),
            pltpu.VMEM((2, HEADS, rows), F32),
            pltpu.VMEM((rows, 2 * rows), F32),
            pltpu.VMEM((micro, HEADS, rows, 2 * rows), F32),
            side_rows,
            side_rows,
            pltpu.VMEM((micro, width, rows), F32),
            turned,
            turned,
            pltpu.VMEM((micro, rows // SIDE, width), BF16),
            pltpu.VMEM((micro, rows // SIDE, width), BF16),
            pltpu.VMEM((micro, step, rows), BF16),
            pltpu.VMEM((micro, step, rows), BF16),
            dma((4,)), dma((2, width // HEAD)),
            dma((2,)), dma((2,)),
            dma((SIDE,)), dma((1,)),
            dma((1,)), dma((1,)),
            dma((1,)), dma((SIDE,)),
            dma((2, 2)), dma((2, 2)),
            dma((1,)), dma((1,)),
            dma((2, 3)), dma((2, 3)),
            dma((2, 2, 2, 4)), dma((2, 2, 2, 4)),
            dma((2, CHUNKS)),
            dma((2, 2, CHUNKS)), dma((2, 2, CHUNKS)),
            dma((2,)), dma((2,)),
            dma((2, 2)), dma((2, 2)),
            dma((2,)), dma((2,)),
            dma((2, SIDE)), dma((2,)),
            dma((2,)), dma((2,)),
            dma((2,)), dma((2, SIDE)),
            pltpu.SemaphoreType.REGULAR,
            pltpu.SemaphoreType.REGULAR,
        ],
        compiler_params=pltpu.CompilerParams(
            collective_id=0, has_side_effects=True, vmem_limit_bytes=60 * 2**20
        ),
        cost_estimate=pl.CostEstimate(flops=4 * 10**9, bytes_accessed=8 * 2**20, transcendentals=2**19),
        name="backward",
    )(x_saved, queries, keys, value_weight, out_weight, out_grad)


def solution(mesh):
    rows = P("section", None, "seq", None)
    weights = P("section", "seq", None)
    return jax.shard_map(
        per_device,
        mesh=mesh,
        in_specs=(rows, rows, rows, weights, weights, P(None, "seq", None)),
        out_specs=(rows, rows, rows),
        check_vma=False,
    )
```

```python
import functools
import math

import jax
import jax.numpy as jnp
from jax import lax
from jax.experimental import pallas as pl
from jax.experimental.pallas import tpu as pltpu
from jax.sharding import PartitionSpec as P

MESH = pl.DeviceIdType.MESH
HEADS = 8
HEAD = 128
ROWS = 128
SIDE = 4
CHUNKS = 4
BF16 = jnp.bfloat16
F32 = jnp.float32
NN = (((1,), (0,)), ((), ()))
NT = (((1,), (1,)), ((), ()))


def dot(left, right, dims=NN):
    return lax.dot_general(left, right, dims, preferred_element_type=F32)


def kernel(
    sections, blocks, width,
    x, q, k, wv, wo, og,
    sg, dq, dk,
    w, qv, kv, xv, ogv, qnext, kt, vals, xh, xmirror, weight, prob, grx, out, skip, acc, vgi, vg,
    stat, statrx, factor, bias, dprob, delta, deltarx, dqown, dqnext, dqrx, pass1, pass2, pass3, pass4,
    lsem, wsem, qsend, qrecv, e1send, e1recv, e2send, e2recv, e3send, e3recv, tsend, trecv, msend, mrecv, zsend, zrecv, rsend, rrecv, isend,
    gsend, grecv, ssend, srecv, esend, erecv, dsend, drecv, f1send, f1recv, f2send, f2recv, f3send, f3recv, go_z, go_r,
):
    s = lax.axis_index("section")
    i = lax.axis_index("seq")
    cy = lax.div(i, SIDE * SIDE)
    cz = lax.rem(lax.div(i, SIDE), SIDE)
    cx = lax.rem(i, SIDE)
    after = lax.rem(i + 1, blocks)
    before = lax.rem(i + blocks - 1, blocks)
    top = sections - 1
    half = sections // 2
    mirror_s = top - s
    step = width // CHUNKS
    per = step // HEAD
    scale = 1.0 / math.sqrt(HEAD)

    def at(y, z, x_):
        return y * (SIDE * SIDE) + z * SIDE + x_

    def copy(src, dst, send, recv, device):
        return pltpu.make_async_remote_copy(
            src_ref=src, dst_ref=dst, send_sem=send, recv_sem=recv,
            device_id=device, device_id_type=MESH,
        )


    def local_copy(n):
        src, dst = ((q.at[0], qv), (k.at[0], kv), (x.at[0], xv), (og, ogv))[n]
        return pltpu.make_async_copy(src, dst, lsem.at[n])


    def shard_copy(a, b):
        src = (wo if a == 0 else wv).at[0, :, pl.ds(b * HEAD, HEAD)]
        return pltpu.make_async_copy(src, w.at[a, cy, cz, cx, b], wsem.at[a, b])

    def columns_of(part, first, count, rows):
        blocks_of = [part(first + n).reshape(rows, HEAD) for n in range(count)]
        return jnp.concatenate(blocks_of, 1)

    def query_copy(m):
        return copy(q.at[0, m], qnext.at[m], qsend.at[m], qrecv.at[m], (s, before))


    quarter = ROWS // SIDE
    back = lax.rem(i + blocks - SIDE, blocks)

    def edge_out(j):
        src = q.at[0, :, pl.ds(j * quarter, quarter)]
        return copy(src, pass1, e1send.at[j], e1recv.at[0], (s, i + j))

    def edge_over(first, last):
        src = q.at[0, :, pl.ds(0, quarter)] if first else pass1
        if last:
            dst, sem = qnext.at[:, pl.ds((SIDE - 1) * quarter, quarter)], e3recv.at[SIDE - 1]
        else:
            dst, sem = pass2, e2recv.at[0]
        return copy(src, dst, e2send.at[0], sem, (s, back))

    def edge_in():
        rows = pl.ds(pl.multiple_of(cx * quarter, quarter), quarter)
        to = i - cx + SIDE - 1
        return copy(pass2, qnext.at[:, rows], e3send.at[0], e3recv.at[cx], (s, to))

    def edge_arrival(j):
        part = qnext.at[:, pl.ds(j * quarter, quarter)]
        return copy(part, part, e3send.at[0], e3recv.at[j], (s, i))

    def stat_copy(m, side):
        to = before if side == 0 else after
        return copy(
            stat.at[m, side], statrx.at[m, 1 - side], tsend.at[m, side], trecv.at[m, 1 - side], (s, to)
        )

    def delta_copy(m, side):
        to = before if side == 0 else after
        return copy(
            delta.at[m, side], deltarx.at[m, 1 - side], esend.at[m, side], erecv.at[m, 1 - side], (s, to)
        )

    def mirror_copy():
        return copy(x.at[0], xmirror, msend.at[0], mrecv.at[0], (mirror_s, i))

    def z_copy(a, d):
        to = at(cy, lax.rem(cz + d, SIDE), cx)
        piece = w.at[a, cy, cz, cx]
        return copy(piece, piece, zsend.at[a, d - 1], zrecv.at[a, d - 1], (s, to))

    def z_arrival(a, d):
        piece = w.at[a, cy, lax.rem(cz + SIDE - d, SIDE), cx]
        return copy(piece, piece, zsend.at[a, d - 1], zrecv.at[a, d - 1], (s, i))

    def slab(a, h, phase, c, part):
        zs = pl.ds(2 * h, 2) if part is None else 2 * h + part
        if phase == 0:
            return w.at[a, cy, zs, c] if h == 0 else w.at[a, c, zs, cx]
        return w.at[a, c, zs] if h == 0 else w.at[a, :, zs, c]

    def kinds(h, phase):
        return (2,) if phase == h else (2, 3)

    def ring(a, h, phase, kind, arrival=False):
        along_x = phase == h
        me = cx if along_x else cy
        plus, minus = lax.rem(me + 1, SIDE), lax.rem(me + SIDE - 1, SIDE)
        across = lax.rem(me + 2, SIDE)
        part = None if kind < 2 or along_x else kind - 2
        if arrival:
            held = (minus, plus, across, across)[kind]
        else:
            held = (me, me, minus, plus)[kind]
        goes = plus if kind % 2 == 0 else minus
        to = at(cy, cz, goes) if along_x else at(goes, cz, cx)
        piece = slab(a, h, phase, held, part)
        sems = (a, h, phase, kind)
        return copy(piece, piece, rsend.at[sems], rrecv.at[sems], (s, to))

    def init_copy(m, c):
        return copy(
            grx.at[m, 0, c], grx.at[m, 1, c], isend.at[m, c], grecv.at[m, 1, c], (s, before)
        )

    def grad_copy(m, c, j):
        to = (s - 1, i) if j == 0 else (s - 1, before)
        return copy(out.at[m, c], grx.at[m, j, c], gsend.at[m, j, c], grecv.at[m, j, c], to)

    def skip_copy(m):
        return copy(out.at[m], skip.at[m], ssend.at[m], srecv.at[m], (mirror_s, i))

    def dq_copy(m):
        return copy(dqnext.at[m], dqrx.at[m], dsend.at[m], drecv.at[m], (s, after))


    ahead = lax.rem(i + SIDE, blocks)

    def dq_part(ref, m, j):
        return ref.at[m, pl.ds(j * step, step)]

    def dq_out(m, j):
        to = i - SIDE + 1 + j
        return copy(dq_part(dqnext, m, j), pass3.at[m], f1send.at[m, j], f1recv.at[m], (s, to))

    def dq_over(m, first, last):
        src = dq_part(dqnext, m, SIDE - 1) if first else pass3.at[m]
        if last:
            return copy(src, dq_part(dqrx, m, 0), f2send.at[m], f3recv.at[m, 0], (s, ahead))
        return copy(src, pass4.at[m], f2send.at[m], f2recv.at[m], (s, ahead))

    def dq_in(m):
        rows = pl.ds(pl.multiple_of(cx * step, step), step)
        return copy(pass4.at[m], dqrx.at[m, rows], f3send.at[m], f3recv.at[m, cx], (s, i - cx))

    def dq_arrival(m, j):
        part = dq_part(dqrx, m, j)
        return copy(part, part, f3send.at[m], f3recv.at[m, j], (s, i))

    for a in range(2):
        for b in range(width // HEAD):
            shard_copy(a, b).start()
    for n in range(3):
        local_copy(n).start()

    @pl.when(s == top)
    def _():
        local_copy(3).start()


    barrier = pltpu.get_barrier_semaphore()

    def greet(section, seq):
        pl.semaphore_signal(barrier, inc=1, device_id=(section, seq), device_id_type=MESH)

    greet(s, after)
    greet(s, before)
    greet(mirror_s, i)
    for d in range(1, SIDE):
        greet(s, at(cy, lax.rem(cz + d, SIDE), cx))
        greet(s, at(cy, cz, lax.rem(cx + d, SIDE)))
    for d in (1, SIDE - 1):
        greet(s, at(lax.rem(cy + d, SIDE), cz, cx))
        greet(s, lax.rem(i + d * SIDE + (blocks - SIDE * SIDE if d > 1 else 0), blocks))

    @pl.when(s > 0)
    def _():
        greet(s - 1, i)
        greet(s - 1, before)

    @pl.when(s < top)
    def _():
        greet(s + 1, i)
        greet(s + 1, after)

    @pl.when(s > 1)
    def _():
        greet(s - 2, i)

    @pl.when(s < top - 1)
    def _():
        greet(s + 2, i)

    odd = lax.rem(s, 2) == 1
    peers = 13 + lax.div(s + 6, sections) + lax.div(2 * top - 1 - s, sections) + 2 * lax.div(s + top, sections) + 2 * lax.div(2 * top - s, sections)
    pl.semaphore_wait(barrier, peers)


    row = lax.broadcasted_iota(jnp.int32, (ROWS, 2 * ROWS), 0)
    col = lax.broadcasted_iota(jnp.int32, (ROWS, 2 * ROWS), 1)
    no_next = jnp.where(i == blocks - 1, 2 * ROWS, 0)
    allowed = ((col < ROWS) & (row <= col)) | ((col >= ROWS) & (row > col - ROWS + no_next))
    bias[...] = jnp.where(allowed, 0.0, -1e30)

    def each_head(body):
        for h in range(HEADS):
            body(h, slice(h * HEAD, (h + 1) * HEAD))

    def soft_in(m):
        @pl.when(cx < SIDE - 1)
        def _():
            query_copy(m).wait_recv()

        def head(h, cols):
            keys = kv[m, :, cols]
            queries = jnp.concatenate([qv[m, :, cols], qnext[m, :, cols]], 0)
            score = dot(keys, queries, NT) * scale + bias[...]
            high = jnp.maximum(jnp.max(score, axis=0, keepdims=True), -1e29)
            e = jnp.exp(score - high)
            total = jnp.sum(e, axis=0, keepdims=True)
            weight[m, h] = e
            one = slice(h, h + 1)
            stat[m, 0, 0, one] = high[:, :ROWS]
            stat[m, 1, 0, one] = high[:, ROWS:]
            stat[m, 0, 1, one] = total[:, :ROWS]
            stat[m, 1, 1, one] = total[:, ROWS:]
            kt[m, cols] = keys.T

        each_head(head)
        for side in range(2):
            stat_copy(m, side).start()

    def soft_out(m):
        for side in range(2):
            stat_copy(m, 1 - side).wait_recv()
            here, there = stat[m, side, 0], statrx[m, side, 0]
            high = jnp.maximum(here, there)
            mine = jnp.exp(here - high)
            total = stat[m, side, 1] * mine + statrx[m, side, 1] * jnp.exp(there - high)
            factor[side] = mine / total

        def head(h, cols):
            one = slice(h, h + 1)
            part = jnp.concatenate([factor[0, one], factor[1, one]], 1)
            p = (weight[m, h] * part).astype(BF16)
            prob[m, h, 0] = p[:, :ROWS]
            prob[m, h, 1] = p[:, ROWS:]

        each_head(head)

    def values():
        @pl.when(s >= half)
        def _():
            mirror_copy().wait_recv()
            xh[...] = (xv[...].astype(F32) + xmirror[...].astype(F32)).astype(BF16)

        @pl.when(s < half)
        def _():
            xh[...] = xv[...]

        def columns(c, carry):
            part = columns_of(lambda b: w[1, :, :, :, b], c * per, per, width)
            result = dot(xh[...].reshape(2 * ROWS, width), part).astype(BF16)
            for m in range(2):
                for u in range(per):
                    block = result[m * ROWS:(m + 1) * ROWS, u * HEAD:(u + 1) * HEAD]
                    vals[m, c * per + u] = block
            return carry

        lax.fori_loop(0, CHUNKS, columns, 0)

    def chain_in(m):
        acc[...] = jnp.zeros_like(acc)

        @pl.when((s < top) & (lax.rem(s, 2) == 0))
        def _():
            for c in range(CHUNKS):
                grad_copy(m, c, 0).wait_recv()

        @pl.when((s < top) & (lax.rem(s, 2) == 1))
        def _():
            for c in range(CHUNKS):
                grad_copy(m, c, 0).wait_recv()
                init_copy(m, c).start()

        def chunk(c, carry):
            grad_copy(m, c, 1).wait_recv()
            both = jnp.concatenate([grx[m, 0, c], grx[m, 1, c]], 1)
            part = columns_of(lambda b: w[0, :, :, :, b], c * per, per, width)
            acc[...] += dot(part, both)
            return carry

        lax.fori_loop(0, CHUNKS, chunk, 0)
        vgi[m, 0] = acc[:, :ROWS].astype(BF16)
        vgi[m, 1] = acc[:, ROWS:].astype(BF16)

    def chain_out(m):
        for h in range(HEADS):
            rows = slice(h * HEAD, (h + 1) * HEAD)
            grad = jnp.concatenate([vgi[m, 0, rows], vgi[m, 1, rows]], 1)
            p = jnp.concatenate([prob[m, h, 0], prob[m, h, 1]], 1)
            vg[rows] = dot(grad, p, NT).astype(BF16)

        @pl.when(s < half - 1)
        def _():
            skip_copy(m).wait_recv()

        @pl.when(s == half - 1)
        def _():
            skip[m] = grx[m, 0]

        def chunk(c, carry):
            part = columns_of(lambda b: w[1, c, :, :, b], 0, width // HEAD, step)
            total = dot(part, vg[...]) + grx[m, 0, c].astype(F32) + skip[m, c].astype(F32)
            out[m, c] = total.astype(BF16)

            @pl.when(lax.rem(s, 2) == 1)
            def _():
                grad_copy(m, c, 1).start()

            @pl.when(s > 0)
            def _():
                grad_copy(m, c, 0).start()

            return carry

        lax.fori_loop(0, CHUNKS, chunk, 0)

        @pl.when(s > half)
        def _():
            skip_copy(m).start()

    def post_in(m):
        def head(h, cols):
            both = jnp.concatenate([vgi[m, 0, cols], vgi[m, 1, cols]], 1)
            grad = dot(vals[m, h], both)
            dprob[m, h] = grad
            p = jnp.concatenate([prob[m, h, 0], prob[m, h, 1]], 1).astype(F32)
            total = jnp.sum(p * grad, axis=0, keepdims=True)
            one = slice(h, h + 1)
            delta[m, 0, one] = total[:, :ROWS]
            delta[m, 1, one] = total[:, ROWS:]

        each_head(head)
        for side in range(2):
            delta_copy(m, side).start()

    def post_out(m):
        for side in range(2):
            delta_copy(m, 1 - side).wait_recv()
            factor[side] = delta[m, side] + deltarx[m, side]

        def head(h, cols):
            one = slice(h, h + 1)
            whole = jnp.concatenate([factor[0, one], factor[1, one]], 1)
            p = jnp.concatenate([prob[m, h, 0], prob[m, h, 1]], 1).astype(F32)
            ds = (p * (dprob[m, h] - whole) * scale).astype(BF16)
            queries = jnp.concatenate([qv[m, :, cols], qnext[m, :, cols]], 0)
            dk[0, m, :, cols] = dot(ds, queries).astype(BF16)
            both = dot(kt[m, cols], ds)
            dqown[m, cols] = both[:, :ROWS]
            dqnext[m, cols] = both[:, ROWS:].astype(BF16)

        each_head(head)

        @pl.when(cx < SIDE - 1)
        def _():
            dq_copy(m).start()

        @pl.when(cx == SIDE - 1)
        def _():
            for j in range(SIDE - 1):
                dq_out(m, j).start()
            dq_over(m, True, False).start()


    def relay(a, phase):
        for h in range(2):
            for kind in range(2):
                ring(a, h, phase, kind, True).wait_recv()
                if kind + 2 in kinds(h, phase):
                    ring(a, h, phase, kind + 2).start()

    def settle(a, phase):
        for h in range(2):
            for kind in kinds(h, phase):
                ring(a, h, phase, kind, True).wait_recv()

    def second():
        for a in range(2):
            settle(a, 0)
            for h in range(2):
                for kind in range(2):
                    ring(a, h, 1, kind).start()

    def each_micro(body):
        def turn(m, carry):
            body(m)
            return carry

        lax.fori_loop(0, 2, turn, 0)

    def start_queries():
        @pl.when(cx == 0)
        def _():
            for j in range(1, SIDE):
                edge_out(j).start()
            edge_over(True, False).start()

        @pl.when(cx > 0)
        def _():
            for m in range(2):
                query_copy(m).start()

    def edge_first():
        @pl.when(cx > 0)
        def _():
            edge_out(0).wait_recv()

        @pl.when((cx > 0) & (cx < SIDE - 1))
        def _():
            edge_over(False, False).start()

        @pl.when(cx == SIDE - 1)
        def _():
            edge_over(False, True).start()

    def edge_second():
        @pl.when(cx < SIDE - 1)
        def _():
            edge_over(False, False).wait_recv()
            edge_in().start()

    @pl.when(s < top - 1)
    def _():
        pl.semaphore_wait(go_z, 1)

    for a in range(2):
        for b in range(width // HEAD):
            shard_copy(a, b).wait()
        for d in range(1, SIDE):
            z_copy(a, d).start()

    start_queries()

    for n in range(3):
        local_copy(n).wait()

    for a in range(2):
        for d in range(1, SIDE):
            z_arrival(a, d).wait_recv()
        for h in range(2):
            for kind in range(2):
                ring(a, h, 0, kind).start()

    @pl.when(s > 1)
    def _():
        pl.semaphore_signal(go_z, inc=1, device_id=(s - 2, i), device_id_type=MESH)

    edge_first()

    for a in range(2):
        relay(a, 0)

    edge_second()

    @pl.when(odd)
    def _():
        second()
        for a in range(2):
            relay(a, 1)
        pl.semaphore_signal(go_r, inc=1, device_id=(s - 1, i), device_id_type=MESH)

    @pl.when(s == top)
    def _():
        local_copy(3).wait()
        for m in range(2):
            for c in range(CHUNKS):
                grx[m, 0, c] = ogv[m, :, c * step:(c + 1) * step].T
                init_copy(m, c).start()

    @pl.when(s >= half)
    def _():
        skip[...] = jnp.zeros_like(skip)

    @pl.when(jnp.logical_not(odd))
    def _():
        pl.semaphore_wait(go_r, 1)
        second()

    @pl.when(cx == SIDE - 1)
    def _():
        for j in range(SIDE):
            edge_arrival(j).wait_recv()

    each_micro(soft_in)

    each_micro(soft_out)

    @pl.when(jnp.logical_not(odd))
    def _():
        for a in range(2):
            relay(a, 1)

    settle(0, 1)
    settle(1, 1)

    @pl.when(s < half)
    def _():
        mirror_copy().start()

    def turn(t, carry):
        m = lax.rem(t, 2)
        early = (t < 2) & (s == 0)

        @pl.when(((t == 0) & (s < half)) | ((t == 2) & (s >= half)))
        def _():
            values()

        @pl.when(t < 2)
        def _():
            chain_in(m)

        @pl.when(early | ((t >= 2) & (t < 4) & (s > 0)))
        def _():
            post_in(m)

        @pl.when(t < 2)
        def _():
            chain_out(m)

        @pl.when(early | ((t >= 4) & (s > 0)))
        def _():
            post_out(m)

        return carry

    lax.fori_loop(0, 6, turn, 0)

    for m in range(2):
        @pl.when(cx < SIDE - 1)
        def _():
            dq_out(m, 0).wait_recv()

        @pl.when((cx > 0) & (cx < SIDE - 1))
        def _():
            dq_over(m, False, False).start()

        @pl.when(cx == 0)
        def _():
            dq_over(m, False, True).start()

    for m in range(2):
        @pl.when(cx > 0)
        def _():
            dq_over(m, False, False).wait_recv()
            dq_in(m).start()

    for m in range(2):
        for c in range(CHUNKS):
            sg[0, m, :, c * step:(c + 1) * step] = out[m, c].T
    for m in range(2):
        @pl.when(cx > 0)
        def _():
            dq_copy(m).wait_recv()

        @pl.when(cx == 0)
        def _():
            for j in range(SIDE):
                dq_arrival(m, j).wait_recv()

        for c in range(CHUNKS):
            rows = slice(c * step, (c + 1) * step)
            dq[0, m, :, rows] = (dqown[m, rows] + dqrx[m, rows].astype(F32)).astype(BF16).T


    @pl.when(cx == 0)
    def _():
        for j in range(1, SIDE):
            edge_out(j).wait_send()

    @pl.when(cx > 0)
    def _():
        for m in range(2):
            query_copy(m).wait_send()

    edge_over(False, False).wait_send()

    @pl.when(cx < SIDE - 1)
    def _():
        edge_in().wait_send()

    for m in range(2):
        @pl.when(cx < SIDE - 1)
        def _():
            dq_copy(m).wait_send()

        @pl.when(cx == SIDE - 1)
        def _():
            for j in range(SIDE - 1):
                dq_out(m, j).wait_send()

        dq_over(m, False, False).wait_send()

        @pl.when(cx > 0)
        def _():
            dq_in(m).wait_send()

        for side in range(2):
            stat_copy(m, side).wait_send()
            delta_copy(m, side).wait_send()
    for a in range(2):
        for d in range(1, SIDE):
            z_copy(a, d).wait_send()
        for h in range(2):
            for phase in range(2):
                for kind in (0, 1) + kinds(h, phase):
                    ring(a, h, phase, kind).wait_send()

    @pl.when(s < half)
    def _():
        mirror_copy().wait_send()

    @pl.when(odd)
    def _():
        for m in range(2):
            for c in range(CHUNKS):
                init_copy(m, c).wait_send()
                grad_copy(m, c, 1).wait_send()

    @pl.when(s > 0)
    def _():
        for m in range(2):
            for c in range(CHUNKS):
                grad_copy(m, c, 0).wait_send()

    @pl.when(s > half)
    def _():
        for m in range(2):
            skip_copy(m).wait_send()


def per_device(x_saved, queries, keys, value_weight, out_weight, out_grad):
    sections = lax.axis_size("section")
    blocks = lax.axis_size("seq")
    micro, rows, width = out_grad.shape
    shape = jax.ShapeDtypeStruct((1, micro, rows, width), BF16)
    step = width // CHUNKS
    vmem = pl.BlockSpec(memory_space=pltpu.VMEM)
    hbm = pl.BlockSpec(memory_space=pltpu.HBM)
    dma = pltpu.SemaphoreType.DMA
    block = pltpu.VMEM((micro, rows, width), BF16)
    turned = pltpu.VMEM((micro, width, rows), BF16)
    chunks = pltpu.VMEM((micro, CHUNKS, step, rows), BF16)
    side_rows = pltpu.VMEM((micro, 2, HEADS, rows), F32)
    return pl.pallas_call(
        functools.partial(kernel, sections, blocks, width),
        out_shape=(shape, shape, shape),
        in_specs=[hbm] * 6,
        out_specs=(vmem,) * 3,
        scratch_shapes=[
            pltpu.VMEM((2, SIDE, SIDE, SIDE, width // HEAD, width // blocks, HEAD), BF16),
            block,
            block,
            block,
            block,
            block,
            turned,
            pltpu.VMEM((micro, HEADS, rows, HEAD), BF16),
            block,
            block,
            pltpu.VMEM((micro, HEADS, rows, 2 * rows), F32),
            pltpu.VMEM((micro, HEADS, 2, rows, rows), BF16),
            pltpu.VMEM((micro, 2, CHUNKS, step, rows), BF16),
            chunks,
            chunks,
            pltpu.VMEM((width, 2 * rows), F32),
            pltpu.VMEM((micro, 2, width, rows), BF16),
            pltpu.VMEM((width, rows), BF16),
            pltpu.VMEM((micro, 2, 2, HEADS, rows), F32),
            pltpu.VMEM((micro, 2, 2, HEADS, rows), F32),
            pltpu.VMEM((2, HEADS, rows), F32),
            pltpu.VMEM((rows, 2 * rows), F32),
            pltpu.VMEM((micro, HEADS, rows, 2 * rows), F32),
            side_rows,
            side_rows,
            pltpu.VMEM((micro, width, rows), F32),
            turned,
            turned,
            pltpu.VMEM((micro, rows // SIDE, width), BF16),
            pltpu.VMEM((micro, rows // SIDE, width), BF16),
            pltpu.VMEM((micro, step, rows), BF16),
            pltpu.VMEM((micro, step, rows), BF16),
            dma((4,)), dma((2, width // HEAD)),
            dma((2,)), dma((2,)),
            dma((SIDE,)), dma((1,)),
            dma((1,)), dma((1,)),
            dma((1,)), dma((SIDE,)),
            dma((2, 2)), dma((2, 2)),
            dma((1,)), dma((1,)),
            dma((2, 3)), dma((2, 3)),
            dma((2, 2, 2, 4)), dma((2, 2, 2, 4)),
            dma((2, CHUNKS)),
            dma((2, 2, CHUNKS)), dma((2, 2, CHUNKS)),
            dma((2,)), dma((2,)),
            dma((2, 2)), dma((2, 2)),
            dma((2,)), dma((2,)),
            dma((2, SIDE)), dma((2,)),
            dma((2,)), dma((2,)),
            dma((2,)), dma((2, SIDE)),
            pltpu.SemaphoreType.REGULAR,
            pltpu.SemaphoreType.REGULAR,
        ],
        compiler_params=pltpu.CompilerParams(
            collective_id=0, has_side_effects=True, vmem_limit_bytes=60 * 2**20
        ),
        cost_estimate=pl.CostEstimate(flops=4 * 10**9, bytes_accessed=8 * 2**20, transcendentals=2**19),
        name="backward",
    )(x_saved, queries, keys, value_weight, out_weight, out_grad)


def solution(mesh):
    rows = P("section", None, "seq", None)
    weights = P("section", "seq", None)
    return jax.shard_map(
        per_device,
        mesh=mesh,
        in_specs=(rows, rows, rows, weights, weights, P(None, "seq", None)),
        out_specs=(rows, rows, rows),
        check_vma=False,
    )
```
